32 devices in a mesh: gx: 8 (over z, y), gy: 4 (over x, core).
Axes of the slice: x: 2, y: 2, z: 4, core: 2. Of those that a mesh axis runs over, the one named last changes fastest.
Arguments:
- tile_sums: bfloat16 [1024, 5, 8192], P(('gx', 'gy')), may hold values from -180 to 180
- tile_dest: int32 [1024], P(('gx', 'gy')), may hold values from 0 to 31, as said below
- tile_place: int32 [1024], P(('gx', 'gy')), may hold values from 0 to 15
- tile_count: int32 [32], P(('gx', 'gy')), may hold values from 16 to 32, as said below
Outputs:
- smoothed: float32 [5, 8, 512, 1024], P(None, 'gx', 'gy')
The draws below stay inside these ranges and needn't reach their ends.
Inputs may be any that keep to these rules, and one draw needn't show every extreme that they name: `tile_dest`: each DEM device's 32 records name every filter device exactly once. Only the first tile_count[d] slots of device d are live; some device has all 32 live and some has half.
All inputs are finite; a program needn't handle non-finite values.
Results may differ from the reference program's by a relative error of at most 0.0003.
Values may be sent and summed in bfloat16 or wider, within the bound.
A program may use at most 192 MiB of HBM per device.

```python
import math
import jax
import jax.numpy as jnp
from jax import lax

NF = 5
TE = 32
BX = 4
BY = 4
RADIUS = 4
NZ = 8
TCELLS = 8192
SLOTS = 32
RECORDS = 1024
N_GX = 8
N_GY = 4
DEVICES = 32


def draw_tile_dest(key, part):
    score_key, favour_key = jax.random.split(jax.random.fold_in(key, 11))
    columns = jnp.arange(DEVICES, dtype=jnp.int32)
    scores = jax.random.randint(score_key, (DEVICES, DEVICES), 0, 65536, dtype=jnp.int32) * DEVICES + columns[None, :]
    favour = jax.random.randint(favour_key, (DEVICES,), 0, 4, dtype=jnp.int32) * (16384 * DEVICES)
    ranked = jnp.argsort(-(scores + favour[None, :]), axis=1, stable=True)
    return ranked[:, :SLOTS].reshape(DEVICES * SLOTS).astype(jnp.int32)


def draw_tile_count(key, part):
    first_key, second_key, third_key = jax.random.split(jax.random.fold_in(key, 23), 3)
    counts = jax.random.randint(first_key, (DEVICES,), SLOTS // 2, SLOTS + 1, dtype=jnp.int32)
    fullest = jax.random.randint(second_key, (), 0, DEVICES, dtype=jnp.int32)
    emptiest = (fullest + 1 + jax.random.randint(third_key, (), 0, DEVICES - 1, dtype=jnp.int32)) % DEVICES
    positions = jnp.arange(DEVICES, dtype=jnp.int32)
    counts = jnp.where(positions == fullest, SLOTS, counts)
    counts = jnp.where(positions == emptiest, SLOTS // 2, counts)
    return counts.astype(jnp.int32)


def touch_ends(array, key, smallest, high):
    longest = array.shape.index(max(array.shape))
    spots = []
    for shift in (0, 1):
        where = [jax.random.randint(jax.random.fold_in(key, axis), (), 0, length) for axis, length in enumerate(array.shape)]
        where[longest] = (where[longest] + shift) % array.shape[longest]
        spots.append(tuple(where))
    return array.at[spots[0]].set(smallest).at[spots[1]].set(high)


def block_levels(rng, dims, pieces, low, largest):
    gain = 1.0
    for dim, shards_of in pieces:
        heights = jax.random.uniform(jax.random.fold_in(jax.random.fold_in(rng, 6), dim), (shards_of,), jnp.float32, low / len(pieces), largest / len(pieces))
        gain = gain * jnp.repeat(jnp.exp(heights), dims[dim] // shards_of).reshape((-1,) + (1,) * (len(dims) - 1 - dim))
    return gain


def gaussian(rng, extent, scale, reach, cuts=(), kind=jnp.bfloat16):
    loudness = block_levels(rng, extent, cuts, -0.22, 0.18) if cuts else 1.0
    entries = jax.random.normal(rng, extent, jnp.float32) * scale * loudness
    return jnp.minimum(jnp.maximum(entries, -reach), reach).astype(kind)


def setup_inputs(seed: int = 0) -> dict:
    keys = jax.random.split(jax.random.key(seed), 5)
    return {
        "tile_sums": gaussian(keys[0], (RECORDS, NF, TCELLS), 30.0, 180.0, ((0, 32),)),
        "tile_dest": draw_tile_dest(jax.random.fold_in(keys[4], 71), 0),
        "tile_place": touch_ends(jax.random.randint(keys[2], (RECORDS,), 0, BX * BY), jax.random.fold_in(keys[2], 1), 0, (BX * BY) - 1).astype(jnp.int32),
        "tile_count": draw_tile_count(jax.random.fold_in(keys[4], 71), 0),
    }


def gauss_taps():
    spread = RADIUS * 5.0 / 16.0
    raw_taps = [math.exp(-(offset * offset) / (2.0 * spread * spread)) for offset in range(-RADIUS, RADIUS + 1)]
    total_weight = sum(raw_taps)
    return [value / total_weight for value in raw_taps]


def smooth_axis(field, axis, taps):
    length = field.shape[axis]
    widths = [(0, 0)] * field.ndim
    widths[axis] = (RADIUS, RADIUS)
    padded = jnp.pad(field, widths)
    result = jnp.zeros_like(field)
    for offset, weight in enumerate(taps):
        result = result + weight * lax.slice_in_dim(padded, offset, offset + length, axis=axis)
    return result


def reference(tile_sums, tile_dest, tile_place, tile_count):
    tiles_across = N_GX * BX
    tiles_down = N_GY * BY
    start_grid = jnp.zeros((tiles_down, tiles_across, NF, TCELLS), jnp.float32)
    per_device = tile_sums.reshape(DEVICES, SLOTS, NF, TCELLS)
    dest_table = tile_dest.reshape(DEVICES, SLOTS)
    place_table = tile_place.reshape(DEVICES, SLOTS)

    def add_device(grid, element):
        records, target, placed, counted = element
        is_live = jnp.arange(SLOTS, dtype=jnp.int32) < counted
        tile_rows = (target % N_GY) * BY + placed // BX
        tile_cols = (target // N_GY) * BX + placed % BX
        masked = jnp.where(is_live[:, None, None], records.astype(jnp.float32), jnp.float32(0.0))
        return grid.at[tile_rows, tile_cols].add(masked), None

    grid, unused = lax.scan(add_device, start_grid, (per_device, dest_table, place_table, tile_count))
    grid = grid.reshape(tiles_down, tiles_across, NF, NZ, TE, TE)
    deposited = grid.transpose(2, 3, 0, 4, 1, 5).reshape(NF, NZ, tiles_down * TE, tiles_across * TE)
    taps = gauss_taps()

    def smooth_field(field):
        along_x = smooth_axis(field, 2, taps)
        along_y = smooth_axis(along_x, 1, taps)
        return smooth_axis(along_y, 0, taps)

    return lax.map(smooth_field, deposited)
```

```python
import functools
import math

import jax
import jax.numpy as jnp
from jax import lax
from jax.experimental import pallas as pl
from jax.experimental.pallas import tpu as pltpu
from jax.sharding import PartitionSpec as P

TE = 32
BX = 4
BY = 4
RADIUS = 4
TILES = BX * BY
AREA = TE * TE
LANES = 128
ROWS = 16
VMEM_BYTES = 58 * 1024 * 1024


def gauss_taps():
    spread = RADIUS * 5.0 / 16.0
    raw_taps = [
        math.exp(-(offset * offset) / (2.0 * spread * spread))
        for offset in range(-RADIUS, RADIUS + 1)
    ]
    total_weight = sum(raw_taps)
    return [value / total_weight for value in raw_taps]


TAPS = gauss_taps()[RADIUS:]


def filter_list(values, first, count):
    products = {}
    results = []
    for k in range(count):
        total = None
        for j, value in enumerate(values):
            reach = abs(first + j - k)
            if reach > RADIUS:
                continue
            if (j, reach) not in products:
                products[j, reach] = value * TAPS[reach]
            term = products[j, reach]
            total = term if total is None else total + term
        results.append(total)
    return results


def encode_kernel(across, down, planes, sums_ref, dest_ref, place_ref, count_ref, send_ref, picked, smoothed, head):
    fields, slots, cells = sums_ref.shape
    parts = ROWS // across
    width = AREA // parts
    peers = across * down
    row = lax.broadcasted_iota(jnp.int32, (peers, slots), 0)
    slot = lax.broadcasted_iota(jnp.int32, (peers, slots), 1)
    target = (row % across) * down + row // across
    chosen = (dest_ref[...] == target) & (slot < count_ref[...])
    pick = jnp.where(chosen, 1.0, 0.0).astype(jnp.bfloat16)
    place = jnp.sum(jnp.where(chosen, place_ref[...] + 1, 0), axis=1, keepdims=True) - 1
    lane = lax.broadcasted_iota(jnp.int32, (across, LANES), 1)
    for column in range(down):
        start = jnp.where(lane == fields, place[column * across : (column + 1) * across], 0)
        for k in range(planes):
            head[k * down + column] = start

    def one_field(f, carry):
        for z in range(planes):
            span = slice(z * AREA, (z + 1) * AREA)
            picked[:, span] = jnp.dot(pick, sums_ref[f, :, span], preferred_element_type=jnp.float32)

        def one_column(column, carry):
            rows = pl.ds(pl.multiple_of(column * across, across), across)
            peaks = [jnp.zeros((across, LANES), jnp.float32)] * planes
            for c in range(AREA // LANES):
                values = [
                    picked[rows, z * AREA + c * LANES : z * AREA + (c + 1) * LANES]
                    for z in range(planes)
                ]
                for k, result in enumerate(filter_list(values, 0, planes)):
                    smoothed[k, :, c * LANES : (c + 1) * LANES] = result
                    peaks[k] = jnp.maximum(peaks[k], jnp.abs(result))
            for k in range(planes):
                peak = jnp.max(peaks[k], axis=1, keepdims=True)
                power = jnp.floor(jnp.log2(jnp.maximum(peak, 1e-30))) + 1.0
                scale = jnp.exp2(15.0 - power)
                code = jnp.clip(jnp.round(smoothed[k] * scale), -32767.0, 32767.0)
                code = jnp.concatenate([code[:, p * width : (p + 1) * width] for p in range(parts)], axis=0)
                where = k * down + column
                send_ref[where, :, pl.ds(pl.multiple_of(f * width, width), width)] = code.astype(
                    jnp.int32
                ).astype(jnp.int16)
                head[where] = jnp.where(lane == f, power.astype(jnp.int32), head[where])
            return carry

        return lax.fori_loop(0, down, one_column, carry)

    lax.fori_loop(0, fields, one_field, 0)
    full = fields * width
    for d in range(peers):
        block = head[d]
        if parts > 1:
            block = jnp.concatenate([block] * parts, axis=0)
        send_ref[d, :, full : full + LANES] = block.astype(jnp.int16)


def along_x(value, lane, row):
    count = value.shape[0]
    after = jnp.where(row == count - 1, 0.0, pltpu.roll(value, count - 1, 0))
    before = jnp.where(row == 0, 0.0, pltpu.roll(value, 1, 0))
    total = value * TAPS[0]
    for k in range(1, RADIUS + 1):
        right = pltpu.roll(jnp.where(lane < k, after, value), LANES - k, 1)
        left = pltpu.roll(jnp.where(lane >= LANES - k, before, value), k, 1)
        total = total + TAPS[k] * (right + left)
    return total


def deposit_kernel(across, fields, code_ref, head_ref, out_ref, tiles):
    f = pl.program_id(0)
    sources = code_ref.shape[0]
    parts = ROWS // across
    width = AREA // parts
    records = sources * across
    head = head_ref[...].astype(jnp.int32)[:, :across].reshape(records, LANES)
    place = head[:, fields : fields + 1]
    lane = lax.broadcasted_iota(jnp.int32, (records, LANES), 1)
    power = jnp.sum(jnp.where(lane == f, head, 0), axis=1, keepdims=True).astype(jnp.float32)
    scale = jnp.exp2(power - 15.0)
    row = lax.broadcasted_iota(jnp.int32, (records, TILES * across), 0)
    column = lax.broadcasted_iota(jnp.int32, (records, TILES * across), 1)
    hit = place * across + row % across == column
    low_land = jnp.where(hit, scale, 0.0).astype(jnp.bfloat16)
    high_land = (low_land.astype(jnp.float32) * 256.0).astype(jnp.bfloat16)
    contract = (((0,), (0,)), ((), ()))
    for p in range(parts):
        code = code_ref[...].astype(jnp.int32).reshape(sources, parts, across, width)[:, p]
        code = code.reshape(records, width)
        high = (code + 128) >> 8
        low = code - high * 256
        tiles[:, p * width : (p + 1) * width] = lax.dot_general(
            high_land, high.astype(jnp.float32).astype(jnp.bfloat16), contract, preferred_element_type=jnp.float32
        ) + lax.dot_general(
            low_land, low.astype(jnp.float32).astype(jnp.bfloat16), contract, preferred_element_type=jnp.float32
        )
    lane = lax.broadcasted_iota(jnp.int32, (across, LANES), 1)
    side = lax.broadcasted_iota(jnp.int32, (across, LANES), 0)

    def one_row(ly, carry):
        for c in range(AREA // LANES):
            cells = [
                tiles[pl.ds(pl.multiple_of((ly * BX + lx) * across, across), across), c * LANES : (c + 1) * LANES]
                for lx in range(BX)
            ]
            for a in range(LANES // TE):
                joined = cells[0] if a == 0 else pltpu.roll(cells[0], LANES - a * TE, 1)
                for lx in range(1, BX):
                    turn = (lx - a) * TE % LANES
                    moved = pltpu.roll(cells[lx], turn, 1) if turn else cells[lx]
                    joined = jnp.where(lane < lx * TE, joined, moved)
                out_ref[0, ly * TE + c * (LANES // TE) + a] = along_x(joined, lane, side)
        return carry

    lax.fori_loop(0, BY, one_row, 0)


def finish_kernel(across, mid_ref, above_ref, below_ref, out_ref, turned):
    height = mid_ref.shape[1]
    step = 8
    for y in range(0, height, step):
        values = []
        for r in range(y - RADIUS, y + step + RADIUS):
            if r < 0:
                values.append(above_ref[0, r + RADIUS])
            elif r >= height:
                values.append(below_ref[0, r - height])
            else:
                values.append(mid_ref[0, r])
        for k, result in enumerate(filter_list(values, -RADIUS, step)):
            turned[(y + k) * across : (y + k + 1) * across, :] = result
        for g in range(across):
            out_ref[0, 0, y : y + step, g * LANES : (g + 1) * LANES] = turned[
                pl.ds(y * across + g, step, stride=across), :
            ]


def local(across, down, tile_sums, tile_dest, tile_place, tile_count):
    slots, fields, cells = tile_sums.shape
    planes = cells // AREA
    peers = across * down
    parts = ROWS // across
    width = AREA // parts
    height = BY * TE
    params = pltpu.CompilerParams(vmem_limit_bytes=VMEM_BYTES)
    vmem = pl.BlockSpec(memory_space=pltpu.VMEM)
    send = pl.pallas_call(
        functools.partial(encode_kernel, across, down, planes),
        out_shape=jax.ShapeDtypeStruct((peers, ROWS, fields * width + LANES), jnp.int16),
        in_specs=[vmem] * 4,
        out_specs=vmem,
        scratch_shapes=[
            pltpu.VMEM((peers, cells), jnp.float32),
            pltpu.VMEM((planes, across, AREA), jnp.float32),
            pltpu.VMEM((peers, across, LANES), jnp.int32),
        ],
        compiler_params=params,
    )(
        tile_sums.transpose(1, 0, 2),
        tile_dest.reshape(1, slots),
        tile_place.reshape(1, slots),
        tile_count.reshape(1, 1),
    )
    got = lax.all_to_all(send, ("gx", "gy"), split_axis=0, concat_axis=0, tiled=True)
    mid = pl.pallas_call(
        functools.partial(deposit_kernel, across, fields),
        grid=(fields,),
        out_shape=jax.ShapeDtypeStruct((fields, height, across, LANES), jnp.float32),
        in_specs=[
            pl.BlockSpec((peers, ROWS, width), lambda f: (0, 0, f)),
            pl.BlockSpec((peers, ROWS, LANES), lambda f: (0, 0, fields * width // LANES)),
        ],
        out_specs=pl.BlockSpec((1, height, across, LANES), lambda f: (f, 0, 0, 0)),
        scratch_shapes=[pltpu.VMEM((TILES * across, AREA), jnp.float32)],
        compiler_params=params,
    )(got, got)
    up = [(i, i + 1) for i in range(down - 1)]
    above = lax.ppermute(mid[:, height - RADIUS :], "gy", up)
    below = lax.ppermute(mid[:, :RADIUS], "gy", [(j, i) for i, j in up])
    edge = pl.BlockSpec((1, RADIUS, across, LANES), lambda f: (f, 0, 0, 0))
    return pl.pallas_call(
        functools.partial(finish_kernel, across),
        grid=(fields,),
        out_shape=jax.ShapeDtypeStruct((fields, 1, height, across * LANES), jnp.float32),
        in_specs=[pl.BlockSpec((1, height, across, LANES), lambda f: (f, 0, 0, 0)), edge, edge],
        out_specs=pl.BlockSpec((1, 1, height, across * LANES), lambda f: (f, 0, 0, 0)),
        scratch_shapes=[pltpu.VMEM((height * across, LANES), jnp.float32)],
        compiler_params=params,
    )(mid, above, below)


def solution(mesh):
    across, down = mesh.shape["gx"], mesh.shape["gy"]
    return jax.shard_map(
        functools.partial(local, across, down),
        mesh=mesh,
        in_specs=(P(("gx", "gy"), None, None), P(("gx", "gy")), P(("gx", "gy")), P(("gx", "gy"))),
        out_specs=P(None, "gx", "gy", None),
        check_vma=False,
    )
```

```python
import functools
import math

import jax
import jax.numpy as jnp
import ml_dtypes
import numpy as np
from jax import lax
from jax.experimental import pallas as pl
from jax.experimental.pallas import tpu as pltpu
from jax.sharding import PartitionSpec as P

TE = 32
BX = 4
BY = 4
RADIUS = 4
TILES = BX * BY
AREA = TE * TE
LANES = 128
ROWS = 16
VMEM_BYTES = 58 * 1024 * 1024


def gauss_taps():
    spread = RADIUS * 5.0 / 16.0
    raw_taps = [
        math.exp(-(offset * offset) / (2.0 * spread * spread))
        for offset in range(-RADIUS, RADIUS + 1)
    ]
    total_weight = sum(raw_taps)
    return [value / total_weight for value in raw_taps]


TAPS = gauss_taps()[RADIUS:]


def filter_list(values, first, count):
    products = {}
    results = []
    for k in range(count):
        total = None
        for j, value in enumerate(values):
            reach = abs(first + j - k)
            if reach > RADIUS:
                continue
            if (j, reach) not in products:
                products[j, reach] = value * TAPS[reach]
            term = products[j, reach]
            total = term if total is None else total + term
        results.append(total)
    return results


def encode_kernel(across, down, planes, sums_ref, dest_ref, place_ref, count_ref, send_ref, picked, smoothed, head):
    fields, slots, cells = sums_ref.shape
    parts = ROWS // across
    width = AREA // parts
    peers = across * down
    row = lax.broadcasted_iota(jnp.int32, (peers, slots), 0)
    slot = lax.broadcasted_iota(jnp.int32, (peers, slots), 1)
    target = (row % across) * down + row // across
    chosen = (dest_ref[...] == target) & (slot < count_ref[...])
    pick = jnp.where(chosen, 1.0, 0.0).astype(jnp.bfloat16)
    place = jnp.sum(jnp.where(chosen, place_ref[...] + 1, 0), axis=1, keepdims=True) - 1
    lane = lax.broadcasted_iota(jnp.int32, (across, LANES), 1)
    for column in range(down):
        start = jnp.where(lane == fields, place[column * across : (column + 1) * across], 0)
        for k in range(planes):
            head[k * down + column] = start

    def one_field(f, carry):
        for z in range(planes):
            span = slice(z * AREA, (z + 1) * AREA)
            picked[:, span] = jnp.dot(pick, sums_ref[f, :, span], preferred_element_type=jnp.float32)

        def one_column(column, carry):
            rows = pl.ds(pl.multiple_of(column * across, across), across)
            peaks = [jnp.zeros((across, LANES), jnp.float32)] * planes
            for c in range(AREA // LANES):
                values = [
                    picked[rows, z * AREA + c * LANES : z * AREA + (c + 1) * LANES]
                    for z in range(planes)
                ]
                for k, result in enumerate(filter_list(values, 0, planes)):
                    smoothed[k, :, c * LANES : (c + 1) * LANES] = result
                    peaks[k] = jnp.maximum(peaks[k], jnp.abs(result))
            for k in range(planes):
                peak = jnp.max(peaks[k], axis=1, keepdims=True)
                power = jnp.floor(jnp.log2(jnp.maximum(peak, 1e-30))) + 1.0
                scale = jnp.exp2(15.0 - power)
                code = jnp.clip(jnp.round(smoothed[k] * scale), -32767.0, 32767.0)
                code = jnp.concatenate([code[:, p * width : (p + 1) * width] for p in range(parts)], axis=0)
                where = k * down + column
                send_ref[where, :, pl.ds(pl.multiple_of(f * width, width), width)] = code.astype(
                    jnp.int32
                ).astype(jnp.int16)
                head[where] = jnp.where(lane == f, power.astype(jnp.int32), head[where])
            return carry

        return lax.fori_loop(0, down, one_column, carry)

    lax.fori_loop(0, fields, one_field, 0)
    full = fields * width
    for d in range(peers):
        block = head[d]
        if parts > 1:
            block = jnp.concatenate([block] * parts, axis=0)
        send_ref[d, :, full : full + LANES] = block.astype(jnp.int16)


def turn_matrix():
    band = np.zeros((BX * TE + 2 * TE, BX * TE))
    taps = gauss_taps()
    for x in range(BX * TE):
        for k in range(-RADIUS, RADIUS + 1):
            source = x + k
            if source < 0:
                source += BX * TE + 2 * TE
            band[source, x] = taps[k + RADIUS]
    per = LANES // TE
    matrix = np.zeros((BX + 1, per, TE, per, BX * TE))
    for a in range(per):
        for lx in range(BX):
            matrix[lx, a, :, a, :] = band[lx * TE : (lx + 1) * TE]
        half = TE // 2
        matrix[BX, a, :half, a, :] = band[BX * TE : BX * TE + half]
        matrix[BX, a, half:, a, :] = band[BX * TE + 2 * TE - half :]
    matrix = matrix.reshape((BX + 1) * LANES, per * BX * TE).astype(np.float32)
    high = matrix.astype(ml_dtypes.bfloat16)
    low = (matrix - high.astype(np.float32)).astype(ml_dtypes.bfloat16)
    return high, low


def land_tiles(across, fields, f, code_ref, head_ref, tiles):
    sources = code_ref.shape[0]
    parts = ROWS // across
    width = AREA // parts
    records = sources * across
    head = head_ref[...].astype(jnp.int32)[:, :across].reshape(records, LANES)
    place = head[:, fields : fields + 1]
    lane = lax.broadcasted_iota(jnp.int32, (records, LANES), 1)
    power = jnp.sum(jnp.where(lane == f, head, 0), axis=1, keepdims=True).astype(jnp.float32)
    scale = jnp.exp2(power - 15.0)
    row = lax.broadcasted_iota(jnp.int32, (records, TILES * across), 0)
    column = lax.broadcasted_iota(jnp.int32, (records, TILES * across), 1)
    hit = place * across + row % across == column
    low_land = jnp.where(hit, scale, 0.0).T.astype(jnp.bfloat16)
    high_land = (low_land.astype(jnp.float32) * 256.0).astype(jnp.bfloat16)
    for p in range(parts):
        code = code_ref[...].astype(jnp.int32).reshape(sources, parts, across, width)[:, p]
        code = code.reshape(records, width)
        high = (code + 128) >> 8
        low = code - high * 256
        tiles[:, p * width : (p + 1) * width] = jnp.dot(
            high_land, high.astype(jnp.float32).astype(jnp.bfloat16), preferred_element_type=jnp.float32
        ) + jnp.dot(low_land, low.astype(jnp.float32).astype(jnp.bfloat16), preferred_element_type=jnp.float32)


def turn_row(across, ly, tiles, turn_high_ref, turn_low_ref):
    lane = lax.broadcasted_iota(jnp.int32, (across, LANES), 1)
    side = lax.broadcasted_iota(jnp.int32, (across, LANES), 0)
    lines = []
    for c in range(AREA // LANES):
        cells = [
            tiles[pl.ds(pl.multiple_of((ly * BX + lx) * across, across), across), c * LANES : (c + 1) * LANES]
            for lx in range(BX)
        ]
        after = jnp.where(side == across - 1, 0.0, pltpu.roll(cells[0], across - 1, 0))
        before = jnp.where(side == 0, 0.0, pltpu.roll(cells[BX - 1], 1, 0))
        cells.append(jnp.where(lane % TE < TE // 2, after, before))
        lines.append(jnp.concatenate(cells, axis=1))
    whole = jnp.concatenate(lines, axis=0)
    high = whole.astype(jnp.bfloat16)
    low = (whole - high.astype(jnp.float32)).astype(jnp.bfloat16)
    return (
        jnp.dot(high, turn_high_ref[...], preferred_element_type=jnp.float32)
        + jnp.dot(low, turn_high_ref[...], preferred_element_type=jnp.float32)
        + jnp.dot(high, turn_low_ref[...], preferred_element_type=jnp.float32)
    )


def deposit_kernel(across, fields, code_ref, head_ref, turn_high_ref, turn_low_ref, out_ref, tiles):
    land_tiles(across, fields, pl.program_id(0), code_ref, head_ref, tiles)
    per = LANES // TE

    def one_row(ly, carry):
        turned = turn_row(across, ly, tiles, turn_high_ref, turn_low_ref)
        for c in range(AREA // LANES):
            for a in range(per):
                out_ref[0, ly * TE + c * per + a] = turned[c * across : (c + 1) * across, a * LANES : (a + 1) * LANES]
        return carry

    lax.fori_loop(0, BY, one_row, 0)


def finish_kernel(across, mid_ref, above_ref, below_ref, out_ref, turned):
    height = mid_ref.shape[1]
    step = 8
    for y in range(0, height, step):
        values = []
        for r in range(y - RADIUS, y + step + RADIUS):
            if r < 0:
                values.append(above_ref[0, r + RADIUS])
            elif r >= height:
                values.append(below_ref[0, r - height])
            else:
                values.append(mid_ref[0, r])
        for k, result in enumerate(filter_list(values, -RADIUS, step)):
            turned[(y + k) * across : (y + k + 1) * across, :] = result
        for g in range(across):
            out_ref[0, 0, y : y + step, g * LANES : (g + 1) * LANES] = turned[
                pl.ds(y * across + g, step, stride=across), :
            ]


def local(across, down, tile_sums, tile_dest, tile_place, tile_count):
    slots, fields, cells = tile_sums.shape
    planes = cells // AREA
    peers = across * down
    parts = ROWS // across
    width = AREA // parts
    height = BY * TE
    params = pltpu.CompilerParams(vmem_limit_bytes=VMEM_BYTES)
    vmem = pl.BlockSpec(memory_space=pltpu.VMEM)
    send = pl.pallas_call(
        functools.partial(encode_kernel, across, down, planes),
        out_shape=jax.ShapeDtypeStruct((peers, ROWS, fields * width + LANES), jnp.int16),
        in_specs=[vmem] * 4,
        out_specs=vmem,
        scratch_shapes=[
            pltpu.VMEM((peers, cells), jnp.float32),
            pltpu.VMEM((planes, across, AREA), jnp.float32),
            pltpu.VMEM((peers, across, LANES), jnp.int32),
        ],
        compiler_params=params,
    )(
        tile_sums.transpose(1, 0, 2),
        tile_dest.reshape(1, slots),
        tile_place.reshape(1, slots),
        tile_count.reshape(1, 1),
    )
    got = lax.all_to_all(send, ("gx", "gy"), split_axis=0, concat_axis=0, tiled=True)
    mid = pl.pallas_call(
        functools.partial(deposit_kernel, across, fields),
        grid=(fields,),
        out_shape=jax.ShapeDtypeStruct((fields, height, across, LANES), jnp.float32),
        in_specs=[
            pl.BlockSpec((peers, ROWS, width), lambda f: (0, 0, f)),
            pl.BlockSpec((peers, ROWS, LANES), lambda f: (0, 0, fields * width // LANES)),
            vmem,
            vmem,
        ],
        out_specs=pl.BlockSpec((1, height, across, LANES), lambda f: (f, 0, 0, 0)),
        scratch_shapes=[pltpu.VMEM((TILES * across, AREA), jnp.float32)],
        compiler_params=params,
    )(got, got, *turn_matrix())
    up = [(i, i + 1) for i in range(down - 1)]
    above = lax.ppermute(mid[:, height - RADIUS :], "gy", up)
    below = lax.ppermute(mid[:, :RADIUS], "gy", [(j, i) for i, j in up])
    edge = pl.BlockSpec((1, RADIUS, across, LANES), lambda f: (f, 0, 0, 0))
    return pl.pallas_call(
        functools.partial(finish_kernel, across),
        grid=(fields,),
        out_shape=jax.ShapeDtypeStruct((fields, 1, height, across * LANES), jnp.float32),
        in_specs=[pl.BlockSpec((1, height, across, LANES), lambda f: (f, 0, 0, 0)), edge, edge],
        out_specs=pl.BlockSpec((1, 1, height, across * LANES), lambda f: (f, 0, 0, 0)),
        scratch_shapes=[pltpu.VMEM((height * across, LANES), jnp.float32)],
        compiler_params=params,
    )(mid, above, below)


def solution(mesh):
    across, down = mesh.shape["gx"], mesh.shape["gy"]
    return jax.shard_map(
        functools.partial(local, across, down),
        mesh=mesh,
        in_specs=(P(("gx", "gy"), None, None), P(("gx", "gy")), P(("gx", "gy")), P(("gx", "gy"))),
        out_specs=P(None, "gx", "gy", None),
        check_vma=False,
    )
```

```python
import functools
import math

import jax
import jax.numpy as jnp
import ml_dtypes
import numpy as np
from jax import lax
from jax.experimental import pallas as pl
from jax.experimental.pallas import tpu as pltpu
from jax.sharding import PartitionSpec as P

TE = 32
BX = 4
BY = 4
RADIUS = 4
TILES = BX * BY
AREA = TE * TE
LANES = 128
ROWS = 16
VMEM_BYTES = 58 * 1024 * 1024


def gauss_taps():
    spread = RADIUS * 5.0 / 16.0
    raw_taps = [
        math.exp(-(offset * offset) / (2.0 * spread * spread))
        for offset in range(-RADIUS, RADIUS + 1)
    ]
    total_weight = sum(raw_taps)
    return [value / total_weight for value in raw_taps]


TAPS = gauss_taps()[RADIUS:]


def filter_list(values, first, count):
    products = {}
    results = []
    for k in range(count):
        total = None
        for j, value in enumerate(values):
            reach = abs(first + j - k)
            if reach > RADIUS:
                continue
            if (j, reach) not in products:
                products[j, reach] = value * TAPS[reach]
            term = products[j, reach]
            total = term if total is None else total + term
        results.append(total)
    return results


def encode_start(across, down, planes, fields, dest_ref, place_ref, count_ref, head):
    peers, slots = across * down, dest_ref.shape[1]
    row = lax.broadcasted_iota(jnp.int32, (peers, slots), 0)
    slot = lax.broadcasted_iota(jnp.int32, (peers, slots), 1)
    target = (row % across) * down + row // across
    chosen = (dest_ref[...] == target) & (slot < count_ref[...])
    place = jnp.sum(jnp.where(chosen, place_ref[...] + 1, 0), axis=1, keepdims=True) - 1
    lane = lax.broadcasted_iota(jnp.int32, (across, LANES), 1)
    for column in range(down):
        start = jnp.where(lane == fields, place[column * across : (column + 1) * across], 0)
        for k in range(planes):
            head[k * down + column] = start
    return jnp.where(chosen, 1.0, 0.0).astype(jnp.bfloat16)


def encode_field(across, down, planes, f, pick, sums_ref, picked, smoothed, head, put):
    parts = ROWS // across
    width = AREA // parts
    lane = lax.broadcasted_iota(jnp.int32, (across, LANES), 1)
    for z in range(planes):
        span = slice(z * AREA, (z + 1) * AREA)
        picked[:, span] = jnp.dot(pick, sums_ref[f, :, span], preferred_element_type=jnp.float32)

    def one_column(column, carry):
        rows = pl.ds(pl.multiple_of(column * across, across), across)
        peaks = [jnp.zeros((across, LANES), jnp.float32)] * planes
        for c in range(AREA // LANES):
            values = [
                picked[rows, z * AREA + c * LANES : z * AREA + (c + 1) * LANES]
                for z in range(planes)
            ]
            for k, result in enumerate(filter_list(values, 0, planes)):
                smoothed[k, :, c * LANES : (c + 1) * LANES] = result
                peaks[k] = jnp.maximum(peaks[k], jnp.abs(result))
        for k in range(planes):
            peak = jnp.max(peaks[k], axis=1, keepdims=True)
            power = jnp.floor(jnp.log2(jnp.maximum(peak, 1e-30))) + 1.0
            scale = jnp.exp2(15.0 - power)
            code = jnp.clip(jnp.round(smoothed[k] * scale), -32767.0, 32767.0)
            code = jnp.concatenate([code[:, p * width : (p + 1) * width] for p in range(parts)], axis=0)
            where = k * down + column
            put(f, where, code.astype(jnp.int32).astype(jnp.int16))
            head[where] = jnp.where(lane == f, power.astype(jnp.int32), head[where])
        return carry

    lax.fori_loop(0, down, one_column, 0)


def full_head(across, block):
    return jnp.concatenate([block] * (ROWS // across), axis=0).astype(jnp.int16)


def encode_kernel(across, down, planes, sums_ref, dest_ref, place_ref, count_ref, send_ref, picked, smoothed, head):
    fields = sums_ref.shape[0]
    width = AREA * across // ROWS
    pick = encode_start(across, down, planes, fields, dest_ref, place_ref, count_ref, head)

    def put(f, where, code):
        send_ref[where, :, pl.ds(pl.multiple_of(f * width, width), width)] = code

    def one_field(f, carry):
        encode_field(across, down, planes, f, pick, sums_ref, picked, smoothed, head, put)
        return carry

    lax.fori_loop(0, fields, one_field, 0)
    full = fields * width
    for d in range(across * down):
        send_ref[d, :, full : full + LANES] = full_head(across, head[d])


def turn_matrix():
    band = np.zeros((BX * TE + 2 * TE, BX * TE))
    taps = gauss_taps()
    for x in range(BX * TE):
        for k in range(-RADIUS, RADIUS + 1):
            source = x + k
            if source < 0:
                source += BX * TE + 2 * TE
            band[source, x] = taps[k + RADIUS]
    per = LANES // TE
    matrix = np.zeros((BX + 1, per, TE, per, BX * TE))
    for a in range(per):
        for lx in range(BX):
            matrix[lx, a, :, a, :] = band[lx * TE : (lx + 1) * TE]
        half = TE // 2
        matrix[BX, a, :half, a, :] = band[BX * TE : BX * TE + half]
        matrix[BX, a, half:, a, :] = band[BX * TE + 2 * TE - half :]
    matrix = matrix.reshape((BX + 1) * LANES, per * BX * TE).astype(np.float32)
    high = matrix.astype(ml_dtypes.bfloat16)
    low = (matrix - high.astype(np.float32)).astype(ml_dtypes.bfloat16)
    return high, low


def land_tiles(across, fields, f, code_ref, head_ref, tiles):
    sources = code_ref.shape[0]
    parts = ROWS // across
    width = AREA // parts
    records = sources * across
    head = head_ref[...].astype(jnp.int32)[:, :across].reshape(records, LANES)
    place = head[:, fields : fields + 1]
    lane = lax.broadcasted_iota(jnp.int32, (records, LANES), 1)
    power = jnp.sum(jnp.where(lane == f, head, 0), axis=1, keepdims=True).astype(jnp.float32)
    scale = jnp.exp2(power - 15.0)
    row = lax.broadcasted_iota(jnp.int32, (records, TILES * across), 0)
    column = lax.broadcasted_iota(jnp.int32, (records, TILES * across), 1)
    hit = place * across + row % across == column
    low_land = jnp.where(hit, scale, 0.0).T.astype(jnp.bfloat16)
    high_land = (low_land.astype(jnp.float32) * 256.0).astype(jnp.bfloat16)
    for p in range(parts):
        code = code_ref[...].astype(jnp.int32).reshape(sources, parts, across, width)[:, p]
        code = code.reshape(records, width)
        high = (code + 128) >> 8
        low = code - high * 256
        tiles[:, p * width : (p + 1) * width] = jnp.dot(
            high_land, high.astype(jnp.float32).astype(jnp.bfloat16), preferred_element_type=jnp.float32
        ) + jnp.dot(low_land, low.astype(jnp.float32).astype(jnp.bfloat16), preferred_element_type=jnp.float32)


def turn_row(across, ly, tiles, turn_high_ref, turn_low_ref):
    lane = lax.broadcasted_iota(jnp.int32, (across, LANES), 1)
    side = lax.broadcasted_iota(jnp.int32, (across, LANES), 0)
    lines = []
    for c in range(AREA // LANES):
        cells = [
            tiles[pl.ds(pl.multiple_of((ly * BX + lx) * across, across), across), c * LANES : (c + 1) * LANES]
            for lx in range(BX)
        ]
        after = jnp.where(side == across - 1, 0.0, pltpu.roll(cells[0], across - 1, 0))
        before = jnp.where(side == 0, 0.0, pltpu.roll(cells[BX - 1], 1, 0))
        cells.append(jnp.where(lane % TE < TE // 2, after, before))
        lines.append(jnp.concatenate(cells, axis=1))
    whole = jnp.concatenate(lines, axis=0)
    high = whole.astype(jnp.bfloat16)
    low = (whole - high.astype(jnp.float32)).astype(jnp.bfloat16)
    return (
        jnp.dot(high, turn_high_ref[...], preferred_element_type=jnp.float32)
        + jnp.dot(low, turn_high_ref[...], preferred_element_type=jnp.float32)
        + jnp.dot(high, turn_low_ref[...], preferred_element_type=jnp.float32)
    )


def deposit_kernel(across, fields, code_ref, head_ref, turn_high_ref, turn_low_ref, out_ref, tiles):
    land_tiles(across, fields, pl.program_id(0), code_ref, head_ref, tiles)
    per = LANES // TE

    def one_row(ly, carry):
        turned = turn_row(across, ly, tiles, turn_high_ref, turn_low_ref)
        for c in range(AREA // LANES):
            for a in range(per):
                out_ref[0, ly * TE + c * per + a] = turned[c * across : (c + 1) * across, a * LANES : (a + 1) * LANES]
        return carry

    lax.fori_loop(0, BY, one_row, 0)


def exchange_kernel(
    across, down, planes, sums_ref, dest_ref, place_ref, count_ref, turn_high_ref, turn_low_ref,
    mid_ref, above_ref, below_ref, picked, smoothed, head, send, send_head, got, got_head, tiles, halo,
    send_sem, recv_sem, own_sem, halo_send_sem, halo_recv_sem,
):
    fields = sums_ref.shape[0]
    peers = across * down
    height = mid_ref.shape[1]
    my_x, my_y = lax.axis_index("gx"), lax.axis_index("gy")
    me = my_x * down + my_y

    barrier = pltpu.get_barrier_semaphore()

    def greet(j, carry):
        peer = (me + j) % peers
        pl.semaphore_signal(
            barrier, inc=1, device_id=(peer // down, peer % down), device_id_type=pl.DeviceIdType.MESH
        )
        return carry

    lax.fori_loop(1, peers, greet, 0)

    def post(source, target, sem):
        def one(j, carry):
            peer = (me + j) % peers
            pltpu.make_async_remote_copy(
                src_ref=source.at[peer],
                dst_ref=target.at[me],
                send_sem=send_sem.at[sem],
                recv_sem=recv_sem.at[sem],
                device_id=(peer // down, peer % down),
                device_id_type=pl.DeviceIdType.MESH,
            ).start()
            return carry

        lax.fori_loop(1, peers, one, 0)
        pltpu.make_async_copy(source.at[me], target.at[me], own_sem.at[sem]).start()

    def arrived(source, target, sem):
        rest = pl.ds(0, peers - 1)
        pltpu.make_async_copy(source.at[rest], target.at[rest], send_sem.at[sem]).wait()
        pltpu.make_async_copy(source.at[rest], target.at[rest], recv_sem.at[sem]).wait()
        pltpu.make_async_copy(source.at[me], target.at[me], own_sem.at[sem]).wait()

    pick = encode_start(across, down, planes, fields, dest_ref, place_ref, count_ref, head)

    def put(f, where, code):
        send[f, where] = code

    def encode(f, carry):
        encode_field(across, down, planes, f, pick, sums_ref, picked, smoothed, head, put)
        return carry

    encode(0, 0)
    pl.semaphore_wait(barrier, peers - 1)
    post(send.at[0], got.at[0], 0)
    lax.fori_loop(1, fields, encode, 0)
    for d in range(peers):
        send_head[d] = full_head(across, head[d])
    post(send_head, got_head, fields)

    def post_field(f, carry):
        post(send.at[f], got.at[f], f)
        return carry

    lax.fori_loop(1, fields, post_field, 0)

    def to_before(f):
        return pltpu.make_async_remote_copy(
            src_ref=mid_ref.at[f, pl.ds(0, RADIUS)],
            dst_ref=halo.at[1, f],
            send_sem=halo_send_sem.at[1, f],
            recv_sem=halo_recv_sem.at[1, f],
            device_id=(my_x, my_y - 1),
            device_id_type=pl.DeviceIdType.MESH,
        )

    def to_after(f):
        return pltpu.make_async_remote_copy(
            src_ref=mid_ref.at[f, pl.ds(height - RADIUS, RADIUS)],
            dst_ref=halo.at[0, f],
            send_sem=halo_send_sem.at[0, f],
            recv_sem=halo_recv_sem.at[0, f],
            device_id=(my_x, my_y + 1),
            device_id_type=pl.DeviceIdType.MESH,
        )

    arrived(send_head, got_head, fields)
    per = LANES // TE

    def deposit(f, carry):
        arrived(send.at[f], got.at[f], f)
        land_tiles(across, fields, f, got.at[f], got_head, tiles)

        def one_row(ly, inner):
            turned = turn_row(across, ly, tiles, turn_high_ref, turn_low_ref)
            for c in range(AREA // LANES):
                for a in range(per):
                    mid_ref[f, ly * TE + c * per + a] = turned[
                        c * across : (c + 1) * across, a * LANES : (a + 1) * LANES
                    ]
            return inner

        lax.fori_loop(0, BY, one_row, 0)

        @pl.when(my_y > 0)
        def _():
            to_before(f).start()

        @pl.when(my_y < down - 1)
        def _():
            to_after(f).start()

        return carry

    lax.fori_loop(0, fields, deposit, 0)

    @pl.when(my_y > 0)
    def _():
        def one(f, carry):
            to_before(f).wait_send()
            to_after(f).wait_recv()
            return carry

        lax.fori_loop(0, fields, one, 0)
        above_ref[...] = halo[0]

    @pl.when(my_y == 0)
    def _():
        above_ref[...] = jnp.zeros_like(above_ref)

    @pl.when(my_y < down - 1)
    def _():
        def one(f, carry):
            to_after(f).wait_send()
            to_before(f).wait_recv()
            return carry

        lax.fori_loop(0, fields, one, 0)
        below_ref[...] = halo[1]

    @pl.when(my_y == down - 1)
    def _():
        below_ref[...] = jnp.zeros_like(below_ref)


def finish_kernel(across, mid_ref, above_ref, below_ref, out_ref, turned):
    height = mid_ref.shape[1]
    step = 8
    for y in range(0, height, step):
        values = []
        for r in range(y - RADIUS, y + step + RADIUS):
            if r < 0:
                values.append(above_ref[0, r + RADIUS])
            elif r >= height:
                values.append(below_ref[0, r - height])
            else:
                values.append(mid_ref[0, r])
        for k, result in enumerate(filter_list(values, -RADIUS, step)):
            turned[(y + k) * across : (y + k + 1) * across, :] = result
        for g in range(across):
            out_ref[0, 0, y : y + step, g * LANES : (g + 1) * LANES] = turned[
                pl.ds(y * across + g, step, stride=across), :
            ]


def by_exchange(across, down, planes, fields, operands):
    peers = across * down
    width = AREA * across // ROWS
    height = BY * TE
    vmem = pl.BlockSpec(memory_space=pltpu.VMEM)
    return pl.pallas_call(
        functools.partial(exchange_kernel, across, down, planes),
        out_shape=[
            jax.ShapeDtypeStruct((fields, height, across, LANES), jnp.float32),
            jax.ShapeDtypeStruct((fields, RADIUS, across, LANES), jnp.float32),
            jax.ShapeDtypeStruct((fields, RADIUS, across, LANES), jnp.float32),
        ],
        in_specs=[vmem] * 6,
        out_specs=[vmem] * 3,
        scratch_shapes=[
            pltpu.VMEM((peers, planes * AREA), jnp.float32),
            pltpu.VMEM((planes, across, AREA), jnp.float32),
            pltpu.VMEM((peers, across, LANES), jnp.int32),
            pltpu.VMEM((fields, peers, ROWS, width), jnp.int16),
            pltpu.VMEM((peers, ROWS, LANES), jnp.int16),
            pltpu.VMEM((fields, peers, ROWS, width), jnp.int16),
            pltpu.VMEM((peers, ROWS, LANES), jnp.int16),
            pltpu.VMEM((TILES * across, AREA), jnp.float32),
            pltpu.VMEM((2, fields, RADIUS, across, LANES), jnp.float32),
            pltpu.SemaphoreType.DMA((fields + 1,)),
            pltpu.SemaphoreType.DMA((fields + 1,)),
            pltpu.SemaphoreType.DMA((fields + 1,)),
            pltpu.SemaphoreType.DMA((2, fields)),
            pltpu.SemaphoreType.DMA((2, fields)),
        ],
        compiler_params=pltpu.CompilerParams(
            vmem_limit_bytes=VMEM_BYTES, collective_id=0, has_side_effects=True
        ),
    )(*operands, *turn_matrix())


def by_all_to_all(across, down, planes, fields, operands):
    peers = across * down
    width = AREA * across // ROWS
    height = BY * TE
    params = pltpu.CompilerParams(vmem_limit_bytes=VMEM_BYTES)
    vmem = pl.BlockSpec(memory_space=pltpu.VMEM)
    send = pl.pallas_call(
        functools.partial(encode_kernel, across, down, planes),
        out_shape=jax.ShapeDtypeStruct((peers, ROWS, fields * width + LANES), jnp.int16),
        in_specs=[vmem] * 4,
        out_specs=vmem,
        scratch_shapes=[
            pltpu.VMEM((peers, planes * AREA), jnp.float32),
            pltpu.VMEM((planes, across, AREA), jnp.float32),
            pltpu.VMEM((peers, across, LANES), jnp.int32),
        ],
        compiler_params=params,
    )(*operands)
    got = lax.all_to_all(send, ("gx", "gy"), split_axis=0, concat_axis=0, tiled=True)
    mid = pl.pallas_call(
        functools.partial(deposit_kernel, across, fields),
        grid=(fields,),
        out_shape=jax.ShapeDtypeStruct((fields, height, across, LANES), jnp.float32),
        in_specs=[
            pl.BlockSpec((peers, ROWS, width), lambda f: (0, 0, f)),
            pl.BlockSpec((peers, ROWS, LANES), lambda f: (0, 0, fields * width // LANES)),
            vmem,
            vmem,
        ],
        out_specs=pl.BlockSpec((1, height, across, LANES), lambda f: (f, 0, 0, 0)),
        scratch_shapes=[pltpu.VMEM((TILES * across, AREA), jnp.float32)],
        compiler_params=params,
    )(got, got, *turn_matrix())
    up = [(i, i + 1) for i in range(down - 1)]
    above = lax.ppermute(mid[:, height - RADIUS :], "gy", up)
    below = lax.ppermute(mid[:, :RADIUS], "gy", [(j, i) for i, j in up])
    return mid, above, below


def local(across, down, tile_sums, tile_dest, tile_place, tile_count):
    slots, fields, cells = tile_sums.shape
    planes = cells // AREA
    height = BY * TE
    operands = (
        tile_sums.transpose(1, 0, 2),
        tile_dest.reshape(1, slots),
        tile_place.reshape(1, slots),
        tile_count.reshape(1, 1),
    )
    fits = 8 * fields * slots * cells < VMEM_BYTES
    plan = by_exchange if fits else by_all_to_all
    mid, above, below = plan(across, down, planes, fields, operands)
    edge = pl.BlockSpec((1, RADIUS, across, LANES), lambda f: (f, 0, 0, 0))
    return pl.pallas_call(
        functools.partial(finish_kernel, across),
        grid=(fields,),
        out_shape=jax.ShapeDtypeStruct((fields, 1, height, across * LANES), jnp.float32),
        in_specs=[pl.BlockSpec((1, height, across, LANES), lambda f: (f, 0, 0, 0)), edge, edge],
        out_specs=pl.BlockSpec((1, 1, height, across * LANES), lambda f: (f, 0, 0, 0)),
        scratch_shapes=[pltpu.VMEM((height * across, LANES), jnp.float32)],
        compiler_params=pltpu.CompilerParams(vmem_limit_bytes=VMEM_BYTES),
    )(mid, above, below)


def solution(mesh):
    across, down = mesh.shape["gx"], mesh.shape["gy"]
    return jax.shard_map(
        functools.partial(local, across, down),
        mesh=mesh,
        in_specs=(P(("gx", "gy"), None, None), P(("gx", "gy")), P(("gx", "gy")), P(("gx", "gy"))),
        out_specs=P(None, "gx", "gy", None),
        check_vma=False,
    )
```

```python
import functools
import math

import jax
import jax.numpy as jnp
import ml_dtypes
import numpy as np
from jax import lax
from jax.experimental import pallas as pl
from jax.experimental.pallas import tpu as pltpu
from jax.sharding import PartitionSpec as P

TE = 32
BX = 4
BY = 4
RADIUS = 4
TILES = BX * BY
AREA = TE * TE
LANES = 128
ROWS = 16
VMEM_BYTES = 58 * 1024 * 1024


def gauss_taps():
    spread = RADIUS * 5.0 / 16.0
    raw_taps = [
        math.exp(-(offset * offset) / (2.0 * spread * spread))
        for offset in range(-RADIUS, RADIUS + 1)
    ]
    total_weight = sum(raw_taps)
    return [value / total_weight for value in raw_taps]


TAPS = gauss_taps()[RADIUS:]


def filter_list(values, first, count):
    products = {}
    results = []
    for k in range(count):
        total = None
        for j, value in enumerate(values):
            reach = abs(first + j - k)
            if reach > RADIUS:
                continue
            if (j, reach) not in products:
                products[j, reach] = value * TAPS[reach]
            term = products[j, reach]
            total = term if total is None else total + term
        results.append(total)
    return results


def head_spot(across):
    lane = lax.broadcasted_iota(jnp.int32, (across, LANES), 1)
    row = lax.broadcasted_iota(jnp.int32, (across, LANES), 0)
    return jnp.where(lane // 8 == row, lane % 8, -1)


def encode_start(across, down, planes, fields, dest_ref, place_ref, count_ref, head):
    peers, slots = across * down, dest_ref.shape[1]
    row = lax.broadcasted_iota(jnp.int32, (peers, slots), 0)
    slot = lax.broadcasted_iota(jnp.int32, (peers, slots), 1)
    target = (row % across) * down + row // across
    chosen = (dest_ref[...] == target) & (slot < count_ref[...])
    place = jnp.sum(jnp.where(chosen, place_ref[...] + 1, 0), axis=1, keepdims=True) - 1
    spot = head_spot(across)
    for column in range(down):
        start = jnp.where(spot == fields, place[column * across : (column + 1) * across], 0)
        for k in range(planes):
            head[k * down + column] = start
    return jnp.where(chosen, 1.0, 0.0).astype(jnp.bfloat16)


def encode_field(across, down, planes, f, pick, sums_ref, picked, smoothed, head, put, first=0, after=None):
    parts = ROWS // across
    width = AREA // parts
    spot = head_spot(across)
    for z in range(planes):
        span = slice(z * AREA, (z + 1) * AREA)
        picked[:, span] = jnp.dot(pick, sums_ref[f, :, span], preferred_element_type=jnp.float32)

    def one_column(index, carry):
        column = (index + first) % down
        rows = pl.ds(pl.multiple_of(column * across, across), across)
        peaks = [jnp.zeros((across, LANES), jnp.float32)] * planes
        for c in range(AREA // LANES):
            values = [
                picked[rows, z * AREA + c * LANES : z * AREA + (c + 1) * LANES]
                for z in range(planes)
            ]
            for k, result in enumerate(filter_list(values, 0, planes)):
                smoothed[k, :, c * LANES : (c + 1) * LANES] = result
                peaks[k] = jnp.maximum(peaks[k], jnp.abs(result))
        for k in range(planes):
            peak = jnp.max(peaks[k], axis=1, keepdims=True)
            power = jnp.floor(jnp.log2(jnp.maximum(peak, 1e-30))) + 1.0
            scale = jnp.exp2(15.0 - power)
            code = jnp.clip(jnp.round(smoothed[k] * scale), -32767.0, 32767.0)
            code = jnp.concatenate([code[:, p * width : (p + 1) * width] for p in range(parts)], axis=0)
            where = k * down + column
            put(f, where, code.astype(jnp.int32).astype(jnp.int16))
            head[where] = jnp.where(spot == f, power.astype(jnp.int32), head[where])
        if after is not None:
            after(column)
        return carry

    lax.fori_loop(0, down, one_column, 0)


def full_head(across, block):
    return jnp.concatenate([block] * (ROWS // across), axis=0).astype(jnp.int16)


def encode_kernel(across, down, planes, sums_ref, dest_ref, place_ref, count_ref, send_ref, picked, smoothed, head):
    fields = sums_ref.shape[0]
    width = AREA * across // ROWS
    pick = encode_start(across, down, planes, fields, dest_ref, place_ref, count_ref, head)

    def put(f, where, code):
        send_ref[where, :, pl.ds(pl.multiple_of(f * width, width), width)] = code

    def one_field(f, carry):
        encode_field(across, down, planes, f, pick, sums_ref, picked, smoothed, head, put)
        return carry

    lax.fori_loop(0, fields, one_field, 0)
    full = fields * width
    for d in range(across * down):
        send_ref[d, :, full : full + LANES] = full_head(across, head[d])


def turn_matrix():
    band = np.zeros((BX * TE + 2 * TE, BX * TE))
    taps = gauss_taps()
    for x in range(BX * TE):
        for k in range(-RADIUS, RADIUS + 1):
            source = x + k
            if source < 0:
                source += BX * TE + 2 * TE
            band[source, x] = taps[k + RADIUS]
    per = LANES // TE
    matrix = np.zeros((BX + 1, per, TE, per, BX * TE))
    for a in range(per):
        for lx in range(BX):
            matrix[lx, a, :, a, :] = band[lx * TE : (lx + 1) * TE]
        half = TE // 2
        matrix[BX, a, :half, a, :] = band[BX * TE : BX * TE + half]
        matrix[BX, a, half:, a, :] = band[BX * TE + 2 * TE - half :]
    matrix = matrix.reshape((BX + 1) * LANES, per * BX * TE).astype(np.float32)
    high = matrix.astype(ml_dtypes.bfloat16)
    low = (matrix - high.astype(np.float32)).astype(ml_dtypes.bfloat16)
    return high, low


def land_tiles(across, fields, f, code_ref, head, tiles):
    sources = code_ref.shape[0]
    parts = ROWS // across
    width = AREA // parts
    records = sources * across
    spot = head_spot(across)[None]
    place = jnp.sum(jnp.where(spot == fields, head, 0), axis=2, keepdims=True).reshape(records, 1)
    power = jnp.sum(jnp.where(spot == f, head, 0), axis=2, keepdims=True).reshape(records, 1).astype(jnp.float32)
    scale = jnp.exp2(power - 15.0)
    row = lax.broadcasted_iota(jnp.int32, (records, TILES * across), 0)
    column = lax.broadcasted_iota(jnp.int32, (records, TILES * across), 1)
    hit = place * across + row % across == column
    low_land = jnp.where(hit, scale, 0.0).T.astype(jnp.bfloat16)
    high_land = (low_land.astype(jnp.float32) * 256.0).astype(jnp.bfloat16)
    for p in range(parts):
        code = code_ref[...].astype(jnp.int32).reshape(sources, parts, across, width)[:, p]
        code = code.reshape(records, width)
        high = (code + 128) >> 8
        low = code - high * 256
        tiles[:, p * width : (p + 1) * width] = jnp.dot(
            high_land, high.astype(jnp.float32).astype(jnp.bfloat16), preferred_element_type=jnp.float32
        ) + jnp.dot(low_land, low.astype(jnp.float32).astype(jnp.bfloat16), preferred_element_type=jnp.float32)


def tile_rows(across, ly, tiles):
    lane = lax.broadcasted_iota(jnp.int32, (across, LANES), 1)
    side = lax.broadcasted_iota(jnp.int32, (across, LANES), 0)
    lines = []
    for c in range(AREA // LANES):
        cells = [
            tiles[pl.ds(pl.multiple_of((ly * BX + lx) * across, across), across), c * LANES : (c + 1) * LANES]
            for lx in range(BX)
        ]
        after = jnp.where(side == across - 1, 0.0, pltpu.roll(cells[0], across - 1, 0))
        before = jnp.where(side == 0, 0.0, pltpu.roll(cells[BX - 1], 1, 0))
        cells.append(jnp.where(lane % TE < TE // 2, after, before))
        lines.append(jnp.concatenate(cells, axis=1))
    whole = jnp.concatenate(lines, axis=0)
    high = whole.astype(jnp.bfloat16)
    return high, (whole - high.astype(jnp.float32)).astype(jnp.bfloat16)


def turn_dot(high, low, turn_high_ref, turn_low_ref):
    return (
        jnp.dot(high, turn_high_ref[...], preferred_element_type=jnp.float32)
        + jnp.dot(low, turn_high_ref[...], preferred_element_type=jnp.float32)
        + jnp.dot(high, turn_low_ref[...], preferred_element_type=jnp.float32)
    )


def deposit_kernel(across, fields, code_ref, head_ref, turn_high_ref, turn_low_ref, out_ref, tiles):
    land_tiles(across, fields, pl.program_id(0), code_ref, head_ref[...].astype(jnp.int32)[:, :across], tiles)
    per = LANES // TE

    def one_row(ly, carry):
        turned = turn_dot(*tile_rows(across, ly, tiles), turn_high_ref, turn_low_ref)
        for c in range(AREA // LANES):
            for a in range(per):
                out_ref[0, ly * TE + c * per + a] = turned[c * across : (c + 1) * across, a * LANES : (a + 1) * LANES]
        return carry

    lax.fori_loop(0, BY, one_row, 0)


def exchange_kernel(
    across, down, planes, sums_hbm, dest_ref, place_ref, count_ref, turn_high_hbm, turn_low_hbm, out_hbm,
    sums, turn_high, turn_low, picked, smoothed, head, send, send_head, got, got_head, tiles, line_high, line_low,
    mid, halo, turned, result, in_sem, out_sem, send_sem, recv_sem, own_sem, halo_send_sem, halo_recv_sem,
):
    fields = sums.shape[0]
    peers = across * down
    height = mid.shape[1]
    my_x, my_y = lax.axis_index("gx"), lax.axis_index("gy")
    me = my_x * down + my_y
    mesh_ids = pl.DeviceIdType.MESH

    def load(f):
        return pltpu.make_async_copy(sums_hbm.at[f], sums.at[f], in_sem.at[f])

    for f in range(fields):
        load(f).start()
    load_high = pltpu.make_async_copy(turn_high_hbm, turn_high, in_sem.at[fields])
    load_low = pltpu.make_async_copy(turn_low_hbm, turn_low, in_sem.at[fields + 1])
    load_high.start()
    load_low.start()

    barrier = pltpu.get_barrier_semaphore()

    def greet(j, carry):
        peer = (me + j) % peers
        pl.semaphore_signal(barrier, inc=1, device_id=(peer // down, peer % down), device_id_type=mesh_ids)
        return carry

    lax.fori_loop(1, peers, greet, 0)

    def push(source, target, sem, x, y):
        pltpu.make_async_remote_copy(
            src_ref=source.at[x * down + y],
            dst_ref=target.at[me],
            send_sem=send_sem.at[sem],
            recv_sem=recv_sem.at[sem],
            device_id=(x, y),
            device_id_type=mesh_ids,
        ).start()

    def post(source, target, sem):
        def one(j, carry):
            peer = (me + 13 * j) % peers
            push(source, target, sem, peer // down, peer % down)
            return carry

        lax.fori_loop(1, peers, one, 0)
        pltpu.make_async_copy(source.at[me], target.at[me], own_sem.at[sem]).start()

    def arrived(source, target, sem):
        rest = pl.ds(0, peers - 1)
        pltpu.make_async_copy(source.at[rest], target.at[rest], send_sem.at[sem]).wait()
        pltpu.make_async_copy(source.at[rest], target.at[rest], recv_sem.at[sem]).wait()
        pltpu.make_async_copy(source.at[me], target.at[me], own_sem.at[sem]).wait()

    @pl.when(my_y == 0)
    def _():
        halo[0] = jnp.zeros(halo.shape[1:], jnp.float32)

    @pl.when(my_y == down - 1)
    def _():
        halo[1] = jnp.zeros(halo.shape[1:], jnp.float32)

    pick = encode_start(across, down, planes, fields, dest_ref, place_ref, count_ref, head)

    def put(f, where, code):
        send[f, where] = code

    def post_column(column):
        def one(j, carry):
            x = (my_x + 3 * j + 4) % across

            @pl.when((x != my_x) | (column != my_y))
            def _():
                push(send.at[0], got.at[0], 0, x, column)

            return carry

        lax.fori_loop(0, across, one, 0)

    def encode(f, carry):
        load(f).wait()
        encode_field(across, down, planes, f, pick, sums, picked, smoothed, head, put)
        return carry

    load(0).wait()
    pl.semaphore_wait(barrier, peers - 1)
    encode_field(across, down, planes, 0, pick, sums, picked, smoothed, head, put, my_y, post_column)
    pltpu.make_async_copy(send.at[0, me], got.at[0, me], own_sem.at[0]).start()
    lax.fori_loop(1, fields, encode, 0)
    for d in range(peers):
        send_head[d] = jnp.sum(head[d], axis=0, keepdims=True)
    post(send_head, got_head, fields)

    def post_field(f, carry):
        post(send.at[f], got.at[f], f)
        return carry

    lax.fori_loop(1, fields, post_field, 0)

    def to_before(f):
        return pltpu.make_async_remote_copy(
            src_ref=mid.at[f, pl.ds(0, RADIUS)],
            dst_ref=halo.at[1, f],
            send_sem=halo_send_sem.at[1, f],
            recv_sem=halo_recv_sem.at[1, f],
            device_id=(my_x, my_y - 1),
            device_id_type=mesh_ids,
        )

    def to_after(f):
        return pltpu.make_async_remote_copy(
            src_ref=mid.at[f, pl.ds(height - RADIUS, RADIUS)],
            dst_ref=halo.at[0, f],
            send_sem=halo_send_sem.at[0, f],
            recv_sem=halo_recv_sem.at[0, f],
            device_id=(my_x, my_y + 1),
            device_id_type=mesh_ids,
        )

    load_high.wait()
    load_low.wait()
    arrived(send_head, got_head, fields)
    per = LANES // TE
    chunks = AREA // LANES
    block = chunks * across
    step = 8

    def write(f, y, values):
        base = pl.multiple_of(y * across, step * across)
        for k, value in enumerate(filter_list(values, -RADIUS, step)):
            turned[pl.ds(base + k * across, across), :] = value
        for g in range(across):
            result[f, 0, pl.ds(pl.multiple_of(y, step), step), g * LANES : (g + 1) * LANES] = turned[
                pl.ds(base + g, step, stride=across), :
            ]

    def store(f):
        return pltpu.make_async_copy(result.at[f], out_hbm.at[f], out_sem.at[f])

    def deposit(f, carry):
        arrived(send.at[f], got.at[f], f)
        heads = jnp.broadcast_to(got_head[...], (peers, across, LANES))
        land_tiles(across, fields, f, got.at[f], heads, tiles)

        for ly in range(BY):
            line_high[ly * block : (ly + 1) * block], line_low[ly * block : (ly + 1) * block] = tile_rows(
                across, ly, tiles
            )
        span = 2 * LANES
        for half in range(per * LANES // span):
            columns = slice(half * span, (half + 1) * span)
            lines = turn_dot(line_high[...], line_low[...], turn_high.at[:, columns], turn_low.at[:, columns])
            for ly in range(BY):
                for c in range(chunks):
                    for a in range(span // LANES):
                        row = ly * block + c * across
                        mid[f, ly * TE + c * per + half * (span // LANES) + a] = lines[
                            row : row + across, a * LANES : (a + 1) * LANES
                        ]

        @pl.when(my_y > 0)
        def _():
            to_before(f).start()

        @pl.when(my_y < down - 1)
        def _():
            to_after(f).start()

        def inner(i, unused):
            write(f, i * step, [mid[f, i * step - RADIUS + r] for r in range(step + 2 * RADIUS)])
            return unused

        lax.fori_loop(1, height // step - 1, inner, 0)

        @pl.when(my_y > 0)
        def _():
            to_before(f).wait_send()
            to_after(f).wait_recv()

        @pl.when(my_y < down - 1)
        def _():
            to_after(f).wait_send()
            to_before(f).wait_recv()

        write(f, 0, [halo[0, f, r] for r in range(RADIUS)] + [mid[f, r] for r in range(step + RADIUS)])
        last = height - step - RADIUS
        write(
            f,
            height - step,
            [mid[f, last + r] for r in range(step + RADIUS)] + [halo[1, f, r] for r in range(RADIUS)],
        )
        store(f).start()
        return carry

    lax.fori_loop(0, fields, deposit, 0)
    for f in range(fields):
        store(f).wait()


def finish_kernel(across, mid_ref, above_ref, below_ref, out_ref, turned):
    height = mid_ref.shape[1]
    step = 8
    for y in range(0, height, step):
        values = []
        for r in range(y - RADIUS, y + step + RADIUS):
            if r < 0:
                values.append(above_ref[0, r + RADIUS])
            elif r >= height:
                values.append(below_ref[0, r - height])
            else:
                values.append(mid_ref[0, r])
        for k, result in enumerate(filter_list(values, -RADIUS, step)):
            turned[(y + k) * across : (y + k + 1) * across, :] = result
        for g in range(across):
            out_ref[0, 0, y : y + step, g * LANES : (g + 1) * LANES] = turned[
                pl.ds(y * across + g, step, stride=across), :
            ]


def by_exchange(across, down, planes, operands):
    fields, slots, cells = operands[0].shape
    peers = across * down
    width = AREA * across // ROWS
    height = BY * TE
    lines = BY * (AREA // LANES) * across
    tables = turn_matrix()
    vmem = pl.BlockSpec(memory_space=pltpu.VMEM)
    hbm = pl.BlockSpec(memory_space=pl.ANY)
    return pl.pallas_call(
        functools.partial(exchange_kernel, across, down, planes),
        out_shape=jax.ShapeDtypeStruct((fields, 1, height, across * LANES), jnp.float32),
        in_specs=[hbm, vmem, vmem, vmem, hbm, hbm],
        out_specs=hbm,
        scratch_shapes=[
            pltpu.VMEM((fields, slots, cells), jnp.bfloat16),
            pltpu.VMEM(tables[0].shape, jnp.bfloat16),
            pltpu.VMEM(tables[1].shape, jnp.bfloat16),
            pltpu.VMEM((peers, planes * AREA), jnp.float32),
            pltpu.VMEM((planes, across, AREA), jnp.float32),
            pltpu.VMEM((peers, across, LANES), jnp.int32),
            pltpu.VMEM((fields, peers, ROWS, width), jnp.int16),
            pltpu.VMEM((peers, 1, LANES), jnp.int32),
            pltpu.VMEM((fields, peers, ROWS, width), jnp.int16),
            pltpu.VMEM((peers, 1, LANES), jnp.int32),
            pltpu.VMEM((TILES * across, AREA), jnp.float32),
            pltpu.VMEM((lines, tables[0].shape[0]), jnp.bfloat16),
            pltpu.VMEM((lines, tables[0].shape[0]), jnp.bfloat16),
            pltpu.VMEM((fields, height, across, LANES), jnp.float32),
            pltpu.VMEM((2, fields, RADIUS, across, LANES), jnp.float32),
            pltpu.VMEM((height * across, LANES), jnp.float32),
            pltpu.VMEM((fields, 1, height, across * LANES), jnp.float32),
            pltpu.SemaphoreType.DMA((fields + 2,)),
            pltpu.SemaphoreType.DMA((fields,)),
            pltpu.SemaphoreType.DMA((fields + 1,)),
            pltpu.SemaphoreType.DMA((fields + 1,)),
            pltpu.SemaphoreType.DMA((fields + 1,)),
            pltpu.SemaphoreType.DMA((2, fields)),
            pltpu.SemaphoreType.DMA((2, fields)),
        ],
        compiler_params=pltpu.CompilerParams(
            vmem_limit_bytes=VMEM_BYTES, collective_id=0, has_side_effects=True
        ),
    )(*operands, *tables)


def by_all_to_all(across, down, planes, fields, operands):
    peers = across * down
    width = AREA * across // ROWS
    height = BY * TE
    params = pltpu.CompilerParams(vmem_limit_bytes=VMEM_BYTES)
    vmem = pl.BlockSpec(memory_space=pltpu.VMEM)
    send = pl.pallas_call(
        functools.partial(encode_kernel, across, down, planes),
        out_shape=jax.ShapeDtypeStruct((peers, ROWS, fields * width + LANES), jnp.int16),
        in_specs=[vmem] * 4,
        out_specs=vmem,
        scratch_shapes=[
            pltpu.VMEM((peers, planes * AREA), jnp.float32),
            pltpu.VMEM((planes, across, AREA), jnp.float32),
            pltpu.VMEM((peers, across, LANES), jnp.int32),
        ],
        compiler_params=params,
    )(*operands)
    got = lax.all_to_all(send, ("gx", "gy"), split_axis=0, concat_axis=0, tiled=True)
    mid = pl.pallas_call(
        functools.partial(deposit_kernel, across, fields),
        grid=(fields,),
        out_shape=jax.ShapeDtypeStruct((fields, height, across, LANES), jnp.float32),
        in_specs=[
            pl.BlockSpec((peers, ROWS, width), lambda f: (0, 0, f)),
            pl.BlockSpec((peers, ROWS, LANES), lambda f: (0, 0, fields * width // LANES)),
            vmem,
            vmem,
        ],
        out_specs=pl.BlockSpec((1, height, across, LANES), lambda f: (f, 0, 0, 0)),
        scratch_shapes=[pltpu.VMEM((TILES * across, AREA), jnp.float32)],
        compiler_params=params,
    )(got, got, *turn_matrix())
    up = [(i, i + 1) for i in range(down - 1)]
    above = lax.ppermute(mid[:, height - RADIUS :], "gy", up)
    below = lax.ppermute(mid[:, :RADIUS], "gy", [(j, i) for i, j in up])
    return mid, above, below


def local(across, down, tile_sums, tile_dest, tile_place, tile_count):
    slots, fields, cells = tile_sums.shape
    planes = cells // AREA
    height = BY * TE
    operands = (
        tile_sums.transpose(1, 0, 2),
        tile_dest.reshape(1, slots),
        tile_place.reshape(1, slots),
        tile_count.reshape(1, 1),
    )
    if 8 * fields * slots * cells < VMEM_BYTES:
        return by_exchange(across, down, planes, operands)
    mid, above, below = by_all_to_all(across, down, planes, fields, operands)
    edge = pl.BlockSpec((1, RADIUS, across, LANES), lambda f: (f, 0, 0, 0))
    return pl.pallas_call(
        functools.partial(finish_kernel, across),
        grid=(fields,),
        out_shape=jax.ShapeDtypeStruct((fields, 1, height, across * LANES), jnp.float32),
        in_specs=[pl.BlockSpec((1, height, across, LANES), lambda f: (f, 0, 0, 0)), edge, edge],
        out_specs=pl.BlockSpec((1, 1, height, across * LANES), lambda f: (f, 0, 0, 0)),
        scratch_shapes=[pltpu.VMEM((height * across, LANES), jnp.float32)],
        compiler_params=pltpu.CompilerParams(vmem_limit_bytes=VMEM_BYTES),
    )(mid, above, below)


def solution(mesh):
    across, down = mesh.shape["gx"], mesh.shape["gy"]
    return jax.shard_map(
        functools.partial(local, across, down),
        mesh=mesh,
        in_specs=(P(("gx", "gy"), None, None), P(("gx", "gy")), P(("gx", "gy")), P(("gx", "gy"))),
        out_specs=P(None, "gx", "gy", None),
        check_vma=False,
    )
```

```python
import functools
import math

import jax
import jax.numpy as jnp
import ml_dtypes
import numpy as np
from jax import lax
from jax.experimental import pallas as pl
from jax.experimental.pallas import tpu as pltpu
from jax.sharding import PartitionSpec as P

TE = 32
BX = 4
BY = 4
RADIUS = 4
TILES = BX * BY
AREA = TE * TE
LANES = 128
ROWS = 16
VMEM_BYTES = 58 * 1024 * 1024


def gauss_taps():
    spread = RADIUS * 5.0 / 16.0
    raw_taps = [
        math.exp(-(offset * offset) / (2.0 * spread * spread))
        for offset in range(-RADIUS, RADIUS + 1)
    ]
    total_weight = sum(raw_taps)
    return [value / total_weight for value in raw_taps]


TAPS = gauss_taps()[RADIUS:]


def filter_list(values, first, count):
    products = {}
    results = []
    for k in range(count):
        total = None
        for j, value in enumerate(values):
            reach = abs(first + j - k)
            if reach > RADIUS:
                continue
            if (j, reach) not in products:
                products[j, reach] = value * TAPS[reach]
            term = products[j, reach]
            total = term if total is None else total + term
        results.append(total)
    return results


def head_spot(across):
    lane = lax.broadcasted_iota(jnp.int32, (across, LANES), 1)
    row = lax.broadcasted_iota(jnp.int32, (across, LANES), 0)
    return jnp.where(lane // 8 == row, lane % 8, -1)


def encode_start(across, down, planes, fields, dest_ref, place_ref, count_ref, head):
    peers, slots = across * down, dest_ref.shape[1]
    row = lax.broadcasted_iota(jnp.int32, (peers, slots), 0)
    slot = lax.broadcasted_iota(jnp.int32, (peers, slots), 1)
    target = (row % across) * down + row // across
    chosen = (dest_ref[...] == target) & (slot < count_ref[...])
    place = jnp.sum(jnp.where(chosen, place_ref[...] + 1, 0), axis=1, keepdims=True) - 1
    spot = head_spot(across)
    for column in range(down):
        start = jnp.where(spot == fields, place[column * across : (column + 1) * across], 0)
        for k in range(planes):
            head[k * down + column] = start
    return jnp.where(chosen, 1.0, 0.0).astype(jnp.bfloat16)


def encode_field(across, down, planes, f, pick, sums_ref, picked, smoothed, head, put, first=0, after=None):
    parts = ROWS // across
    width = AREA // parts
    spot = head_spot(across)
    for z in range(planes):
        span = slice(z * AREA, (z + 1) * AREA)
        picked[:, span] = jnp.dot(pick, sums_ref[f, :, span], preferred_element_type=jnp.float32)

    def one_column(index, carry):
        column = (index + first) % down
        rows = pl.ds(pl.multiple_of(column * across, across), across)
        peaks = [jnp.zeros((across, LANES), jnp.float32)] * planes
        for c in range(AREA // LANES):
            values = [
                picked[rows, z * AREA + c * LANES : z * AREA + (c + 1) * LANES]
                for z in range(planes)
            ]
            for k, result in enumerate(filter_list(values, 0, planes)):
                smoothed[k, :, c * LANES : (c + 1) * LANES] = result
                peaks[k] = jnp.maximum(peaks[k], jnp.abs(result))
        for k in range(planes):
            peak = jnp.max(peaks[k], axis=1, keepdims=True)
            power = jnp.floor(jnp.log2(jnp.maximum(peak, 1e-30))) + 1.0
            scale = jnp.exp2(15.0 - power)
            code = jnp.clip(jnp.round(smoothed[k] * scale), -32767.0, 32767.0)
            code = jnp.concatenate([code[:, p * width : (p + 1) * width] for p in range(parts)], axis=0)
            where = k * down + column
            put(f, where, code.astype(jnp.int32).astype(jnp.int16))
            head[where] = jnp.where(spot == f, power.astype(jnp.int32), head[where])
        if after is not None:
            after(column)
        return carry

    lax.fori_loop(0, down, one_column, 0)


def full_head(across, block):
    return jnp.concatenate([block] * (ROWS // across), axis=0).astype(jnp.int16)


def encode_kernel(across, down, planes, sums_ref, dest_ref, place_ref, count_ref, send_ref, picked, smoothed, head):
    fields = sums_ref.shape[0]
    width = AREA * across // ROWS
    pick = encode_start(across, down, planes, fields, dest_ref, place_ref, count_ref, head)

    def put(f, where, code):
        send_ref[where, :, pl.ds(pl.multiple_of(f * width, width), width)] = code

    def one_field(f, carry):
        encode_field(across, down, planes, f, pick, sums_ref, picked, smoothed, head, put)
        return carry

    lax.fori_loop(0, fields, one_field, 0)
    full = fields * width
    for d in range(across * down):
        send_ref[d, :, full : full + LANES] = full_head(across, head[d])


def turn_matrix():
    band = np.zeros((BX * TE + 2 * TE, BX * TE))
    taps = gauss_taps()
    for x in range(BX * TE):
        for k in range(-RADIUS, RADIUS + 1):
            source = x + k
            if source < 0:
                source += BX * TE + 2 * TE
            band[source, x] = taps[k + RADIUS]
    per = LANES // TE
    matrix = np.zeros((BX + 1, per, TE, per, BX * TE))
    for a in range(per):
        for lx in range(BX):
            matrix[lx, a, :, a, :] = band[lx * TE : (lx + 1) * TE]
        half = TE // 2
        matrix[BX, a, :half, a, :] = band[BX * TE : BX * TE + half]
        matrix[BX, a, half:, a, :] = band[BX * TE + 2 * TE - half :]
    matrix = matrix.reshape((BX + 1) * LANES, per * BX * TE).astype(np.float32)
    high = matrix.astype(ml_dtypes.bfloat16)
    low = (matrix - high.astype(np.float32)).astype(ml_dtypes.bfloat16)
    return high, low


def land_tiles(across, fields, f, code_ref, head, tiles, wait=None):
    sources = code_ref.shape[0]
    parts = ROWS // across
    width = AREA // parts
    records = sources * across
    spot = head_spot(across)[None]
    place = jnp.sum(jnp.where(spot == fields, head, 0), axis=2, keepdims=True).reshape(records, 1)
    power = jnp.sum(jnp.where(spot == f, head, 0), axis=2, keepdims=True).reshape(records, 1).astype(jnp.float32)
    scale = jnp.exp2(power - 15.0)
    row = lax.broadcasted_iota(jnp.int32, (records, TILES * across), 0)
    column = lax.broadcasted_iota(jnp.int32, (records, TILES * across), 1)
    hit = place * across + row % across == column
    low_land = jnp.where(hit, scale, 0.0).T.astype(jnp.bfloat16)
    high_land = (low_land.astype(jnp.float32) * 256.0).astype(jnp.bfloat16)
    if wait is not None:
        wait()
    for p in range(parts):
        code = code_ref[...].astype(jnp.int32).reshape(sources, parts, across, width)[:, p]
        code = code.reshape(records, width)
        high = (code + 128) >> 8
        low = code - high * 256
        tiles[:, p * width : (p + 1) * width] = jnp.dot(
            high_land, high.astype(jnp.float32).astype(jnp.bfloat16), preferred_element_type=jnp.float32
        ) + jnp.dot(low_land, low.astype(jnp.float32).astype(jnp.bfloat16), preferred_element_type=jnp.float32)


def tile_rows(across, ly, tiles):
    lane = lax.broadcasted_iota(jnp.int32, (across, LANES), 1)
    side = lax.broadcasted_iota(jnp.int32, (across, LANES), 0)
    lines = []
    for c in range(AREA // LANES):
        cells = [
            tiles[pl.ds(pl.multiple_of((ly * BX + lx) * across, across), across), c * LANES : (c + 1) * LANES]
            for lx in range(BX)
        ]
        after = jnp.where(side == across - 1, 0.0, pltpu.roll(cells[0], across - 1, 0))
        before = jnp.where(side == 0, 0.0, pltpu.roll(cells[BX - 1], 1, 0))
        cells.append(jnp.where(lane % TE < TE // 2, after, before))
        lines.append(jnp.concatenate(cells, axis=1))
    whole = jnp.concatenate(lines, axis=0)
    high = whole.astype(jnp.bfloat16)
    return high, (whole - high.astype(jnp.float32)).astype(jnp.bfloat16)


def turn_dot(high, low, turn_high_ref, turn_low_ref):
    return (
        jnp.dot(high, turn_high_ref[...], preferred_element_type=jnp.float32)
        + jnp.dot(low, turn_high_ref[...], preferred_element_type=jnp.float32)
        + jnp.dot(high, turn_low_ref[...], preferred_element_type=jnp.float32)
    )


def deposit_kernel(across, fields, code_ref, head_ref, turn_high_ref, turn_low_ref, out_ref, tiles):
    land_tiles(across, fields, pl.program_id(0), code_ref, head_ref[...].astype(jnp.int32)[:, :across], tiles)
    per = LANES // TE

    def one_row(ly, carry):
        turned = turn_dot(*tile_rows(across, ly, tiles), turn_high_ref, turn_low_ref)
        for c in range(AREA // LANES):
            for a in range(per):
                out_ref[0, ly * TE + c * per + a] = turned[c * across : (c + 1) * across, a * LANES : (a + 1) * LANES]
        return carry

    lax.fori_loop(0, BY, one_row, 0)


def exchange_kernel(
    across, down, planes, sums_hbm, dest_ref, place_ref, count_ref, turn_high_hbm, turn_low_hbm, result,
    sums, turn_high, turn_low, picked, smoothed, head, send, send_head, got, got_head, tiles, line_high, line_low,
    mid, halo, turned, in_sem, send_sem, recv_sem, own_sem, halo_send_sem, halo_recv_sem,
):
    fields = sums.shape[0]
    peers = across * down
    height = mid.shape[1]
    my_x, my_y = lax.axis_index("gx"), lax.axis_index("gy")
    me = my_x * down + my_y
    mesh_ids = pl.DeviceIdType.MESH

    def load(f):
        return pltpu.make_async_copy(sums_hbm.at[f], sums.at[f], in_sem.at[f])

    for f in range(fields):
        load(f).start()
    load_high = pltpu.make_async_copy(turn_high_hbm, turn_high, in_sem.at[fields])
    load_low = pltpu.make_async_copy(turn_low_hbm, turn_low, in_sem.at[fields + 1])
    load_high.start()
    load_low.start()

    barrier = pltpu.get_barrier_semaphore()

    def greet(j, carry):
        peer = (me + j) % peers
        pl.semaphore_signal(barrier, inc=1, device_id=(peer // down, peer % down), device_id_type=mesh_ids)
        return carry

    lax.fori_loop(1, peers, greet, 0)

    def push(source, target, sem, x, y):
        pltpu.make_async_remote_copy(
            src_ref=source.at[x * down + y],
            dst_ref=target.at[me],
            send_sem=send_sem.at[sem],
            recv_sem=recv_sem.at[sem],
            device_id=(x, y),
            device_id_type=mesh_ids,
        ).start()

    def post(source, target, sem):
        def one(j, carry):
            peer = (me + 13 * j) % peers
            push(source, target, sem, peer // down, peer % down)
            return carry

        lax.fori_loop(1, peers, one, 0)
        pltpu.make_async_copy(source.at[me], target.at[me], own_sem.at[sem]).start()

    def arrived(source, target, sem):
        rest = pl.ds(0, peers - 1)
        pltpu.make_async_copy(source.at[rest], target.at[rest], send_sem.at[sem]).wait()
        pltpu.make_async_copy(source.at[rest], target.at[rest], recv_sem.at[sem]).wait()
        pltpu.make_async_copy(source.at[me], target.at[me], own_sem.at[sem]).wait()

    @pl.when(my_y == 0)
    def _():
        halo[0] = jnp.zeros(halo.shape[1:], jnp.float32)

    @pl.when(my_y == down - 1)
    def _():
        halo[1] = jnp.zeros(halo.shape[1:], jnp.float32)

    pick = encode_start(across, down, planes, fields, dest_ref, place_ref, count_ref, head)

    def put(f, where, code):
        send[f, where] = code

    def post_column(column):
        def one(j, carry):
            x = (my_x + 3 * j + 4) % across

            @pl.when((x != my_x) | (column != my_y))
            def _():
                push(send.at[0], got.at[0], 0, x, column)

            return carry

        lax.fori_loop(0, across, one, 0)

    def encode(f, carry):
        load(f).wait()
        encode_field(across, down, planes, f, pick, sums, picked, smoothed, head, put)
        return carry

    load(0).wait()
    pl.semaphore_wait(barrier, peers - 1)
    encode_field(across, down, planes, 0, pick, sums, picked, smoothed, head, put, my_y, post_column)
    pltpu.make_async_copy(send.at[0, me], got.at[0, me], own_sem.at[0]).start()
    lax.fori_loop(1, fields, encode, 0)
    for d in range(peers):
        send_head[d] = jnp.sum(head[d], axis=0, keepdims=True)
    post(send_head, got_head, fields)

    def post_field(f, carry):
        post(send.at[f], got.at[f], f)
        return carry

    lax.fori_loop(1, fields, post_field, 0)

    def to_before(f):
        return pltpu.make_async_remote_copy(
            src_ref=mid.at[f, pl.ds(0, RADIUS)],
            dst_ref=halo.at[1, f],
            send_sem=halo_send_sem.at[1, f],
            recv_sem=halo_recv_sem.at[1, f],
            device_id=(my_x, my_y - 1),
            device_id_type=mesh_ids,
        )

    def to_after(f):
        return pltpu.make_async_remote_copy(
            src_ref=mid.at[f, pl.ds(height - RADIUS, RADIUS)],
            dst_ref=halo.at[0, f],
            send_sem=halo_send_sem.at[0, f],
            recv_sem=halo_recv_sem.at[0, f],
            device_id=(my_x, my_y + 1),
            device_id_type=mesh_ids,
        )

    load_high.wait()
    load_low.wait()
    arrived(send_head, got_head, fields)
    per = LANES // TE
    chunks = AREA // LANES
    block = chunks * across
    step = 8

    def write(f, y, values):
        base = pl.multiple_of(y * across, step * across)
        for k, value in enumerate(filter_list(values, -RADIUS, step)):
            turned[pl.ds(base + k * across, across), :] = value
        for g in range(across):
            result[f, 0, pl.ds(pl.multiple_of(y, step), step), g * LANES : (g + 1) * LANES] = turned[
                pl.ds(base + g, step, stride=across), :
            ]

    def deposit(f, carry):
        heads = jnp.broadcast_to(got_head[...], (peers, across, LANES))
        land_tiles(across, fields, f, got.at[f], heads, tiles, lambda: arrived(send.at[f], got.at[f], f))

        for ly in range(BY):
            line_high[ly * block : (ly + 1) * block], line_low[ly * block : (ly + 1) * block] = tile_rows(
                across, ly, tiles
            )
        span = 2 * LANES
        for half in range(per * LANES // span):
            columns = slice(half * span, (half + 1) * span)
            lines = turn_dot(line_high[...], line_low[...], turn_high.at[:, columns], turn_low.at[:, columns])
            for ly in range(BY):
                for c in range(chunks):
                    for a in range(span // LANES):
                        row = ly * block + c * across
                        mid[f, ly * TE + c * per + half * (span // LANES) + a] = lines[
                            row : row + across, a * LANES : (a + 1) * LANES
                        ]

        @pl.when(my_y > 0)
        def _():
            to_before(f).start()

        @pl.when(my_y < down - 1)
        def _():
            to_after(f).start()

        def inner(i, unused):
            write(f, i * step, [mid[f, i * step - RADIUS + r] for r in range(step + 2 * RADIUS)])
            return unused

        lax.fori_loop(1, height // step - 1, inner, 0)

        @pl.when(my_y > 0)
        def _():
            to_before(f).wait_send()
            to_after(f).wait_recv()

        @pl.when(my_y < down - 1)
        def _():
            to_after(f).wait_send()
            to_before(f).wait_recv()

        write(f, 0, [halo[0, f, r] for r in range(RADIUS)] + [mid[f, r] for r in range(step + RADIUS)])
        last = height - step - RADIUS
        write(
            f,
            height - step,
            [mid[f, last + r] for r in range(step + RADIUS)] + [halo[1, f, r] for r in range(RADIUS)],
        )
        return carry

    lax.fori_loop(0, fields, deposit, 0)


def finish_kernel(across, mid_ref, above_ref, below_ref, out_ref, turned):
    height = mid_ref.shape[1]
    step = 8
    for y in range(0, height, step):
        values = []
        for r in range(y - RADIUS, y + step + RADIUS):
            if r < 0:
                values.append(above_ref[0, r + RADIUS])
            elif r >= height:
                values.append(below_ref[0, r - height])
            else:
                values.append(mid_ref[0, r])
        for k, result in enumerate(filter_list(values, -RADIUS, step)):
            turned[(y + k) * across : (y + k + 1) * across, :] = result
        for g in range(across):
            out_ref[0, 0, y : y + step, g * LANES : (g + 1) * LANES] = turned[
                pl.ds(y * across + g, step, stride=across), :
            ]


def by_exchange(across, down, planes, operands):
    fields, slots, cells = operands[0].shape
    peers = across * down
    width = AREA * across // ROWS
    height = BY * TE
    lines = BY * (AREA // LANES) * across
    tables = turn_matrix()
    vmem = pl.BlockSpec(memory_space=pltpu.VMEM)
    hbm = pl.BlockSpec(memory_space=pl.ANY)
    return pl.pallas_call(
        functools.partial(exchange_kernel, across, down, planes),
        out_shape=pltpu.VMEM((fields, 1, height, across * LANES), jnp.float32),
        in_specs=[hbm, vmem, vmem, vmem, hbm, hbm],
        out_specs=vmem,
        scratch_shapes=[
            pltpu.VMEM((fields, slots, cells), jnp.bfloat16),
            pltpu.VMEM(tables[0].shape, jnp.bfloat16),
            pltpu.VMEM(tables[1].shape, jnp.bfloat16),
            pltpu.VMEM((peers, planes * AREA), jnp.float32),
            pltpu.VMEM((planes, across, AREA), jnp.float32),
            pltpu.VMEM((peers, across, LANES), jnp.int32),
            pltpu.VMEM((fields, peers, ROWS, width), jnp.int16),
            pltpu.VMEM((peers, 1, LANES), jnp.int32),
            pltpu.VMEM((fields, peers, ROWS, width), jnp.int16),
            pltpu.VMEM((peers, 1, LANES), jnp.int32),
            pltpu.VMEM((TILES * across, AREA), jnp.float32),
            pltpu.VMEM((lines, tables[0].shape[0]), jnp.bfloat16),
            pltpu.VMEM((lines, tables[0].shape[0]), jnp.bfloat16),
            pltpu.VMEM((fields, height, across, LANES), jnp.float32),
            pltpu.VMEM((2, fields, RADIUS, across, LANES), jnp.float32),
            pltpu.VMEM((height * across, LANES), jnp.float32),
            pltpu.SemaphoreType.DMA((fields + 2,)),
            pltpu.SemaphoreType.DMA((fields + 1,)),
            pltpu.SemaphoreType.DMA((fields + 1,)),
            pltpu.SemaphoreType.DMA((fields + 1,)),
            pltpu.SemaphoreType.DMA((2, fields)),
            pltpu.SemaphoreType.DMA((2, fields)),
        ],
        compiler_params=pltpu.CompilerParams(
            vmem_limit_bytes=VMEM_BYTES // 2, collective_id=0, has_side_effects=True
        ),
    )(*operands, *tables)


def by_all_to_all(across, down, planes, fields, operands):
    peers = across * down
    width = AREA * across // ROWS
    height = BY * TE
    params = pltpu.CompilerParams(vmem_limit_bytes=VMEM_BYTES)
    vmem = pl.BlockSpec(memory_space=pltpu.VMEM)
    send = pl.pallas_call(
        functools.partial(encode_kernel, across, down, planes),
        out_shape=jax.ShapeDtypeStruct((peers, ROWS, fields * width + LANES), jnp.int16),
        in_specs=[vmem] * 4,
        out_specs=vmem,
        scratch_shapes=[
            pltpu.VMEM((peers, planes * AREA), jnp.float32),
            pltpu.VMEM((planes, across, AREA), jnp.float32),
            pltpu.VMEM((peers, across, LANES), jnp.int32),
        ],
        compiler_params=params,
    )(*operands)
    got = lax.all_to_all(send, ("gx", "gy"), split_axis=0, concat_axis=0, tiled=True)
    mid = pl.pallas_call(
        functools.partial(deposit_kernel, across, fields),
        grid=(fields,),
        out_shape=jax.ShapeDtypeStruct((fields, height, across, LANES), jnp.float32),
        in_specs=[
            pl.BlockSpec((peers, ROWS, width), lambda f: (0, 0, f)),
            pl.BlockSpec((peers, ROWS, LANES), lambda f: (0, 0, fields * width // LANES)),
            vmem,
            vmem,
        ],
        out_specs=pl.BlockSpec((1, height, across, LANES), lambda f: (f, 0, 0, 0)),
        scratch_shapes=[pltpu.VMEM((TILES * across, AREA), jnp.float32)],
        compiler_params=params,
    )(got, got, *turn_matrix())
    up = [(i, i + 1) for i in range(down - 1)]
    above = lax.ppermute(mid[:, height - RADIUS :], "gy", up)
    below = lax.ppermute(mid[:, :RADIUS], "gy", [(j, i) for i, j in up])
    return mid, above, below


def local(across, down, tile_sums, tile_dest, tile_place, tile_count):
    slots, fields, cells = tile_sums.shape
    planes = cells // AREA
    height = BY * TE
    operands = (
        tile_sums.transpose(1, 0, 2),
        tile_dest.reshape(1, slots),
        tile_place.reshape(1, slots),
        tile_count.reshape(1, 1),
    )
    if 16 * fields * slots * cells < VMEM_BYTES:
        return by_exchange(across, down, planes, operands)
    mid, above, below = by_all_to_all(across, down, planes, fields, operands)
    edge = pl.BlockSpec((1, RADIUS, across, LANES), lambda f: (f, 0, 0, 0))
    return pl.pallas_call(
        functools.partial(finish_kernel, across),
        grid=(fields,),
        out_shape=jax.ShapeDtypeStruct((fields, 1, height, across * LANES), jnp.float32),
        in_specs=[pl.BlockSpec((1, height, across, LANES), lambda f: (f, 0, 0, 0)), edge, edge],
        out_specs=pl.BlockSpec((1, 1, height, across * LANES), lambda f: (f, 0, 0, 0)),
        scratch_shapes=[pltpu.VMEM((height * across, LANES), jnp.float32)],
        compiler_params=pltpu.CompilerParams(vmem_limit_bytes=VMEM_BYTES),
    )(mid, above, below)


def solution(mesh):
    across, down = mesh.shape["gx"], mesh.shape["gy"]
    return jax.shard_map(
        functools.partial(local, across, down),
        mesh=mesh,
        in_specs=(P(("gx", "gy"), None, None), P(("gx", "gy")), P(("gx", "gy")), P(("gx", "gy"))),
        out_specs=P(None, "gx", "gy", None),
        check_vma=False,
    )
```

```python
import functools
import math

import jax
import jax.numpy as jnp
import ml_dtypes
import numpy as np
from jax import lax
from jax.experimental import pallas as pl
from jax.experimental.pallas import tpu as pltpu
from jax.sharding import PartitionSpec as P

TE = 32
BX = 4
BY = 4
RADIUS = 4
TILES = BX * BY
AREA = TE * TE
LANES = 128
ROWS = 16
VMEM_BYTES = 58 * 1024 * 1024


def gauss_taps():
    spread = RADIUS * 5.0 / 16.0
    raw_taps = [
        math.exp(-(offset * offset) / (2.0 * spread * spread))
        for offset in range(-RADIUS, RADIUS + 1)
    ]
    total_weight = sum(raw_taps)
    return [value / total_weight for value in raw_taps]


TAPS = gauss_taps()[RADIUS:]


def filter_list(values, first, count):
    products = {}
    results = []
    for k in range(count):
        total = None
        for j, value in enumerate(values):
            reach = abs(first + j - k)
            if reach > RADIUS:
                continue
            if (j, reach) not in products:
                products[j, reach] = value * TAPS[reach]
            term = products[j, reach]
            total = term if total is None else total + term
        results.append(total)
    return results


def head_spot(across):
    lane = lax.broadcasted_iota(jnp.int32, (across, LANES), 1)
    row = lax.broadcasted_iota(jnp.int32, (across, LANES), 0)
    return jnp.where(lane // 8 == row, lane % 8, -1)


def encode_start(across, down, planes, fields, dest_ref, place_ref, count_ref, head):
    peers, slots = across * down, dest_ref.shape[1]
    row = lax.broadcasted_iota(jnp.int32, (peers, slots), 0)
    slot = lax.broadcasted_iota(jnp.int32, (peers, slots), 1)
    target = (row % across) * down + row // across
    chosen = (dest_ref[...] == target) & (slot < count_ref[...])
    place = jnp.sum(jnp.where(chosen, place_ref[...] + 1, 0), axis=1, keepdims=True) - 1
    spot = head_spot(across)
    for column in range(down):
        start = jnp.where(spot == fields, place[column * across : (column + 1) * across], 0)
        for k in range(planes):
            head[k * down + column] = start
    return jnp.where(chosen, 1.0, 0.0).astype(jnp.bfloat16)


def encode_field(across, down, planes, f, pick, sums_ref, picked, smoothed, head, put, first=0, ready=None, after=None):
    parts = ROWS // across
    width = AREA // parts
    spot = head_spot(across)
    for z in range(planes):
        span = slice(z * AREA, (z + 1) * AREA)
        picked[:, span] = jnp.dot(pick, sums_ref[f, :, span], preferred_element_type=jnp.float32)

    if ready is not None:
        ready()

    def one_column(index, carry):
        column = (index + first) % down
        rows = pl.ds(pl.multiple_of(column * across, across), across)
        peaks = [jnp.zeros((across, LANES), jnp.float32)] * planes
        for c in range(AREA // LANES):
            values = [
                picked[rows, z * AREA + c * LANES : z * AREA + (c + 1) * LANES]
                for z in range(planes)
            ]
            for k, result in enumerate(filter_list(values, 0, planes)):
                smoothed[k, :, c * LANES : (c + 1) * LANES] = result
                peaks[k] = jnp.maximum(peaks[k], jnp.abs(result))
        for k in range(planes):
            peak = jnp.max(peaks[k], axis=1, keepdims=True)
            power = jnp.floor(jnp.log2(jnp.maximum(peak, 1e-30))) + 1.0
            scale = jnp.exp2(15.0 - power)
            code = jnp.clip(jnp.round(smoothed[k] * scale), -32767.0, 32767.0)
            code = jnp.concatenate([code[:, p * width : (p + 1) * width] for p in range(parts)], axis=0)
            where = k * down + column
            put(f, where, code.astype(jnp.int32).astype(jnp.int16))
            head[where] = jnp.where(spot == f, power.astype(jnp.int32), head[where])
        if after is not None:
            after(column)
        return carry

    lax.fori_loop(0, down, one_column, 0)


def full_head(across, block):
    return jnp.concatenate([block] * (ROWS // across), axis=0).astype(jnp.int16)


def encode_kernel(across, down, planes, sums_ref, dest_ref, place_ref, count_ref, send_ref, picked, smoothed, head):
    fields = sums_ref.shape[0]
    width = AREA * across // ROWS
    pick = encode_start(across, down, planes, fields, dest_ref, place_ref, count_ref, head)

    def put(f, where, code):
        send_ref[where, :, pl.ds(pl.multiple_of(f * width, width), width)] = code

    def one_field(f, carry):
        encode_field(across, down, planes, f, pick, sums_ref, picked, smoothed, head, put)
        return carry

    lax.fori_loop(0, fields, one_field, 0)
    full = fields * width
    for d in range(across * down):
        send_ref[d, :, full : full + LANES] = full_head(across, head[d])


def turn_matrix():
    band = np.zeros((BX * TE + 2 * TE, BX * TE))
    taps = gauss_taps()
    for x in range(BX * TE):
        for k in range(-RADIUS, RADIUS + 1):
            source = x + k
            if source < 0:
                source += BX * TE + 2 * TE
            band[source, x] = taps[k + RADIUS]
    per = LANES // TE
    matrix = np.zeros((BX + 1, per, TE, per, BX * TE))
    for a in range(per):
        for lx in range(BX):
            matrix[lx, a, :, a, :] = band[lx * TE : (lx + 1) * TE]
        half = TE // 2
        matrix[BX, a, :half, a, :] = band[BX * TE : BX * TE + half]
        matrix[BX, a, half:, a, :] = band[BX * TE + 2 * TE - half :]
    matrix = matrix.reshape((BX + 1) * LANES, per * BX * TE).astype(np.float32)
    high = matrix.astype(ml_dtypes.bfloat16)
    low = (matrix - high.astype(np.float32)).astype(ml_dtypes.bfloat16)
    return high, low


def land_tiles(across, fields, f, code_ref, head, tiles, wait=None):
    sources = code_ref.shape[0]
    parts = ROWS // across
    width = AREA // parts
    records = sources * across
    spot = head_spot(across)[None]
    place = jnp.sum(jnp.where(spot == fields, head, 0), axis=2, keepdims=True).reshape(records, 1)
    power = jnp.sum(jnp.where(spot == f, head, 0), axis=2, keepdims=True).reshape(records, 1).astype(jnp.float32)
    scale = jnp.exp2(power - 15.0)
    row = lax.broadcasted_iota(jnp.int32, (records, TILES * across), 0)
    column = lax.broadcasted_iota(jnp.int32, (records, TILES * across), 1)
    hit = place * across + row % across == column
    low_land = jnp.where(hit, scale, 0.0).T.astype(jnp.bfloat16)
    high_land = (low_land.astype(jnp.float32) * 256.0).astype(jnp.bfloat16)
    if wait is not None:
        wait()
    for p in range(parts):
        code = code_ref[...].astype(jnp.int32).reshape(sources, parts, across, width)[:, p]
        code = code.reshape(records, width)
        high = (code + 128) >> 8
        low = code - high * 256
        tiles[:, p * width : (p + 1) * width] = jnp.dot(
            high_land, high.astype(jnp.float32).astype(jnp.bfloat16), preferred_element_type=jnp.float32
        ) + jnp.dot(low_land, low.astype(jnp.float32).astype(jnp.bfloat16), preferred_element_type=jnp.float32)


def tile_rows(across, ly, tiles):
    lane = lax.broadcasted_iota(jnp.int32, (across, LANES), 1)
    side = lax.broadcasted_iota(jnp.int32, (across, LANES), 0)
    lines = []
    for c in range(AREA // LANES):
        cells = [
            tiles[pl.ds(pl.multiple_of((ly * BX + lx) * across, across), across), c * LANES : (c + 1) * LANES]
            for lx in range(BX)
        ]
        after = jnp.where(side == across - 1, 0.0, pltpu.roll(cells[0], across - 1, 0))
        before = jnp.where(side == 0, 0.0, pltpu.roll(cells[BX - 1], 1, 0))
        cells.append(jnp.where(lane % TE < TE // 2, after, before))
        lines.append(jnp.concatenate(cells, axis=1))
    whole = jnp.concatenate(lines, axis=0)
    high = whole.astype(jnp.bfloat16)
    return high, (whole - high.astype(jnp.float32)).astype(jnp.bfloat16)


def turn_dot(high, low, turn_high_ref, turn_low_ref):
    return (
        jnp.dot(high, turn_high_ref[...], preferred_element_type=jnp.float32)
        + jnp.dot(low, turn_high_ref[...], preferred_element_type=jnp.float32)
        + jnp.dot(high, turn_low_ref[...], preferred_element_type=jnp.float32)
    )


def deposit_kernel(across, fields, code_ref, head_ref, turn_high_ref, turn_low_ref, out_ref, tiles):
    land_tiles(across, fields, pl.program_id(0), code_ref, head_ref[...].astype(jnp.int32)[:, :across], tiles)
    per = LANES // TE

    def one_row(ly, carry):
        turned = turn_dot(*tile_rows(across, ly, tiles), turn_high_ref, turn_low_ref)
        for c in range(AREA // LANES):
            for a in range(per):
                out_ref[0, ly * TE + c * per + a] = turned[c * across : (c + 1) * across, a * LANES : (a + 1) * LANES]
        return carry

    lax.fori_loop(0, BY, one_row, 0)


def exchange_kernel(
    across, down, planes, sums_hbm, dest_hbm, place_hbm, count_ref, turn_high_hbm, turn_low_hbm, result,
    sums, dest_ref, place_ref, turn_high, turn_low, picked, smoothed, head, send, send_head, got, got_head, tiles, line_high, line_low,
    mid, halo, turned, in_sem, send_sem, recv_sem, own_sem, halo_send_sem, halo_recv_sem,
):
    fields = sums.shape[0]
    peers = across * down
    height = mid.shape[1]
    my_x, my_y = lax.axis_index("gx"), lax.axis_index("gy")
    me = my_x * down + my_y
    mesh_ids = pl.DeviceIdType.MESH

    def load(f):
        return pltpu.make_async_copy(sums_hbm.at[f], sums.at[f], in_sem.at[f])

    load_dest = pltpu.make_async_copy(dest_hbm, dest_ref, in_sem.at[fields + 2])
    load_place = pltpu.make_async_copy(place_hbm, place_ref, in_sem.at[fields + 3])
    load_dest.start()
    load_place.start()
    for f in range(fields):
        load(f).start()
    load_high = pltpu.make_async_copy(turn_high_hbm, turn_high, in_sem.at[fields])
    load_low = pltpu.make_async_copy(turn_low_hbm, turn_low, in_sem.at[fields + 1])
    load_high.start()
    load_low.start()

    barrier = pltpu.get_barrier_semaphore()

    def greet(j, carry):
        peer = (me + j) % peers
        pl.semaphore_signal(barrier, inc=1, device_id=(peer // down, peer % down), device_id_type=mesh_ids)
        return carry

    lax.fori_loop(1, peers, greet, 0)

    def push(source, target, sem, x, y):
        pltpu.make_async_remote_copy(
            src_ref=source.at[x * down + y],
            dst_ref=target.at[me],
            send_sem=send_sem.at[sem],
            recv_sem=recv_sem.at[sem],
            device_id=(x, y),
            device_id_type=mesh_ids,
        ).start()

    def post(source, target, sem):
        def one(j, carry):
            peer = (me + 13 * j) % peers
            push(source, target, sem, peer // down, peer % down)
            return carry

        lax.fori_loop(1, peers, one, 0)
        pltpu.make_async_copy(source.at[me], target.at[me], own_sem.at[sem]).start()

    def arrived(source, target, sem):
        rest = pl.ds(0, peers - 1)
        pltpu.make_async_copy(source.at[rest], target.at[rest], send_sem.at[sem]).wait()
        pltpu.make_async_copy(source.at[rest], target.at[rest], recv_sem.at[sem]).wait()
        pltpu.make_async_copy(source.at[me], target.at[me], own_sem.at[sem]).wait()

    @pl.when(my_y == 0)
    def _():
        halo[0] = jnp.zeros(halo.shape[1:], jnp.float32)

    @pl.when(my_y == down - 1)
    def _():
        halo[1] = jnp.zeros(halo.shape[1:], jnp.float32)

    load_dest.wait()
    load_place.wait()
    pick = encode_start(across, down, planes, fields, dest_ref, place_ref, count_ref, head)

    def put(f, where, code):
        send[f, where] = code

    def post_column(column):
        def one(j, carry):
            x = (my_x + 3 * j + 4) % across

            @pl.when((x != my_x) | (column != my_y))
            def _():
                push(send.at[0], got.at[0], 0, x, column)

            return carry

        lax.fori_loop(0, across, one, 0)

    def encode(f, carry):
        load(f).wait()
        encode_field(across, down, planes, f, pick, sums, picked, smoothed, head, put)
        return carry

    load(0).wait()
    everyone = lambda: pl.semaphore_wait(barrier, peers - 1)
    encode_field(across, down, planes, 0, pick, sums, picked, smoothed, head, put, my_y, everyone, post_column)
    pltpu.make_async_copy(send.at[0, me], got.at[0, me], own_sem.at[0]).start()
    lax.fori_loop(1, fields, encode, 0)
    for d in range(peers):
        send_head[d] = jnp.sum(head[d], axis=0, keepdims=True)
    post(send_head, got_head, fields)

    def post_field(f, carry):
        post(send.at[f], got.at[f], f)
        return carry

    lax.fori_loop(1, fields, post_field, 0)

    def to_before(f):
        return pltpu.make_async_remote_copy(
            src_ref=mid.at[f, pl.ds(0, RADIUS)],
            dst_ref=halo.at[1, f],
            send_sem=halo_send_sem.at[1, f],
            recv_sem=halo_recv_sem.at[1, f],
            device_id=(my_x, my_y - 1),
            device_id_type=mesh_ids,
        )

    def to_after(f):
        return pltpu.make_async_remote_copy(
            src_ref=mid.at[f, pl.ds(height - RADIUS, RADIUS)],
            dst_ref=halo.at[0, f],
            send_sem=halo_send_sem.at[0, f],
            recv_sem=halo_recv_sem.at[0, f],
            device_id=(my_x, my_y + 1),
            device_id_type=mesh_ids,
        )

    load_high.wait()
    load_low.wait()
    arrived(send_head, got_head, fields)
    per = LANES // TE
    chunks = AREA // LANES
    block = chunks * across
    step = 8

    def write(f, y, values):
        base = pl.multiple_of(y * across, step * across)
        for k, value in enumerate(filter_list(values, -RADIUS, step)):
            turned[pl.ds(base + k * across, across), :] = value
        for g in range(across):
            result[f, 0, pl.ds(pl.multiple_of(y, step), step), g * LANES : (g + 1) * LANES] = turned[
                pl.ds(base + g, step, stride=across), :
            ]

    def deposit(f, carry):
        heads = jnp.broadcast_to(got_head[...], (peers, across, LANES))
        land_tiles(across, fields, f, got.at[f], heads, tiles, lambda: arrived(send.at[f], got.at[f], f))

        for ly in range(BY):
            line_high[ly * block : (ly + 1) * block], line_low[ly * block : (ly + 1) * block] = tile_rows(
                across, ly, tiles
            )
        span = 2 * LANES
        for half in range(per * LANES // span):
            columns = slice(half * span, (half + 1) * span)
            lines = turn_dot(line_high[...], line_low[...], turn_high.at[:, columns], turn_low.at[:, columns])
            for ly in range(BY):
                for c in range(chunks):
                    for a in range(span // LANES):
                        row = ly * block + c * across
                        mid[f, ly * TE + c * per + half * (span // LANES) + a] = lines[
                            row : row + across, a * LANES : (a + 1) * LANES
                        ]

        @pl.when(my_y > 0)
        def _():
            to_before(f).start()

        @pl.when(my_y < down - 1)
        def _():
            to_after(f).start()

        def inner(i, unused):
            write(f, i * step, [mid[f, i * step - RADIUS + r] for r in range(step + 2 * RADIUS)])
            return unused

        lax.fori_loop(1, height // step - 1, inner, 0)

        @pl.when(my_y > 0)
        def _():
            to_before(f).wait_send()
            to_after(f).wait_recv()

        @pl.when(my_y < down - 1)
        def _():
            to_after(f).wait_send()
            to_before(f).wait_recv()

        write(f, 0, [halo[0, f, r] for r in range(RADIUS)] + [mid[f, r] for r in range(step + RADIUS)])
        last = height - step - RADIUS
        write(
            f,
            height - step,
            [mid[f, last + r] for r in range(step + RADIUS)] + [halo[1, f, r] for r in range(RADIUS)],
        )
        return carry

    lax.fori_loop(0, fields, deposit, 0)


def finish_kernel(across, mid_ref, above_ref, below_ref, out_ref, turned):
    height = mid_ref.shape[1]
    step = 8
    for y in range(0, height, step):
        values = []
        for r in range(y - RADIUS, y + step + RADIUS):
            if r < 0:
                values.append(above_ref[0, r + RADIUS])
            elif r >= height:
                values.append(below_ref[0, r - height])
            else:
                values.append(mid_ref[0, r])
        for k, result in enumerate(filter_list(values, -RADIUS, step)):
            turned[(y + k) * across : (y + k + 1) * across, :] = result
        for g in range(across):
            out_ref[0, 0, y : y + step, g * LANES : (g + 1) * LANES] = turned[
                pl.ds(y * across + g, step, stride=across), :
            ]


def by_exchange(across, down, planes, operands):
    fields, slots, cells = operands[0].shape
    peers = across * down
    width = AREA * across // ROWS
    height = BY * TE
    lines = BY * (AREA // LANES) * across
    tables = turn_matrix()
    vmem = pl.BlockSpec(memory_space=pltpu.VMEM)
    hbm = pl.BlockSpec(memory_space=pltpu.HBM)
    return pl.pallas_call(
        functools.partial(exchange_kernel, across, down, planes),
        out_shape=pltpu.VMEM((fields, 1, height, across * LANES), jnp.float32),
        in_specs=[hbm, hbm, hbm, vmem, hbm, hbm],
        out_specs=vmem,
        scratch_shapes=[
            pltpu.VMEM((fields, slots, cells), jnp.bfloat16),
            pltpu.VMEM((1, slots), jnp.int32),
            pltpu.VMEM((1, slots), jnp.int32),
            pltpu.VMEM(tables[0].shape, jnp.bfloat16),
            pltpu.VMEM(tables[1].shape, jnp.bfloat16),
            pltpu.VMEM((peers, planes * AREA), jnp.float32),
            pltpu.VMEM((planes, across, AREA), jnp.float32),
            pltpu.VMEM((peers, across, LANES), jnp.int32),
            pltpu.VMEM((fields, peers, ROWS, width), jnp.int16),
            pltpu.VMEM((peers, 1, LANES), jnp.int32),
            pltpu.VMEM((fields, peers, ROWS, width), jnp.int16),
            pltpu.VMEM((peers, 1, LANES), jnp.int32),
            pltpu.VMEM((TILES * across, AREA), jnp.float32),
            pltpu.VMEM((lines, tables[0].shape[0]), jnp.bfloat16),
            pltpu.VMEM((lines, tables[0].shape[0]), jnp.bfloat16),
            pltpu.VMEM((fields, height, across, LANES), jnp.float32),
            pltpu.VMEM((2, fields, RADIUS, across, LANES), jnp.float32),
            pltpu.VMEM((height * across, LANES), jnp.float32),
            pltpu.SemaphoreType.DMA((fields + 4,)),
            pltpu.SemaphoreType.DMA((fields + 1,)),
            pltpu.SemaphoreType.DMA((fields + 1,)),
            pltpu.SemaphoreType.DMA((fields + 1,)),
            pltpu.SemaphoreType.DMA((2, fields)),
            pltpu.SemaphoreType.DMA((2, fields)),
        ],
        compiler_params=pltpu.CompilerParams(
            vmem_limit_bytes=VMEM_BYTES, collective_id=0, has_side_effects=True
        ),
    )(*operands, *tables)


def by_all_to_all(across, down, planes, fields, operands):
    peers = across * down
    width = AREA * across // ROWS
    height = BY * TE
    params = pltpu.CompilerParams(vmem_limit_bytes=VMEM_BYTES)
    vmem = pl.BlockSpec(memory_space=pltpu.VMEM)
    send = pl.pallas_call(
        functools.partial(encode_kernel, across, down, planes),
        out_shape=jax.ShapeDtypeStruct((peers, ROWS, fields * width + LANES), jnp.int16),
        in_specs=[vmem] * 4,
        out_specs=vmem,
        scratch_shapes=[
            pltpu.VMEM((peers, planes * AREA), jnp.float32),
            pltpu.VMEM((planes, across, AREA), jnp.float32),
            pltpu.VMEM((peers, across, LANES), jnp.int32),
        ],
        compiler_params=params,
    )(*operands)
    got = lax.all_to_all(send, ("gx", "gy"), split_axis=0, concat_axis=0, tiled=True)
    mid = pl.pallas_call(
        functools.partial(deposit_kernel, across, fields),
        grid=(fields,),
        out_shape=jax.ShapeDtypeStruct((fields, height, across, LANES), jnp.float32),
        in_specs=[
            pl.BlockSpec((peers, ROWS, width), lambda f: (0, 0, f)),
            pl.BlockSpec((peers, ROWS, LANES), lambda f: (0, 0, fields * width // LANES)),
            vmem,
            vmem,
        ],
        out_specs=pl.BlockSpec((1, height, across, LANES), lambda f: (f, 0, 0, 0)),
        scratch_shapes=[pltpu.VMEM((TILES * across, AREA), jnp.float32)],
        compiler_params=params,
    )(got, got, *turn_matrix())
    up = [(i, i + 1) for i in range(down - 1)]
    above = lax.ppermute(mid[:, height - RADIUS :], "gy", up)
    below = lax.ppermute(mid[:, :RADIUS], "gy", [(j, i) for i, j in up])
    return mid, above, below


def local(across, down, tile_sums, tile_dest, tile_place, tile_count):
    slots, fields, cells = tile_sums.shape
    planes = cells // AREA
    height = BY * TE
    operands = (
        tile_sums.transpose(1, 0, 2),
        tile_dest.reshape(1, slots),
        tile_place.reshape(1, slots),
        tile_count.reshape(1, 1),
    )
    if 16 * fields * slots * cells < VMEM_BYTES:
        return by_exchange(across, down, planes, operands)
    mid, above, below = by_all_to_all(across, down, planes, fields, operands)
    edge = pl.BlockSpec((1, RADIUS, across, LANES), lambda f: (f, 0, 0, 0))
    return pl.pallas_call(
        functools.partial(finish_kernel, across),
        grid=(fields,),
        out_shape=jax.ShapeDtypeStruct((fields, 1, height, across * LANES), jnp.float32),
        in_specs=[pl.BlockSpec((1, height, across, LANES), lambda f: (f, 0, 0, 0)), edge, edge],
        out_specs=pl.BlockSpec((1, 1, height, across * LANES), lambda f: (f, 0, 0, 0)),
        scratch_shapes=[pltpu.VMEM((height * across, LANES), jnp.float32)],
        compiler_params=pltpu.CompilerParams(vmem_limit_bytes=VMEM_BYTES),
    )(mid, above, below)


def solution(mesh):
    across, down = mesh.shape["gx"], mesh.shape["gy"]
    return jax.shard_map(
        functools.partial(local, across, down),
        mesh=mesh,
        in_specs=(P(("gx", "gy"), None, None), P(("gx", "gy")), P(("gx", "gy")), P(("gx", "gy"))),
        out_specs=P(None, "gx", "gy", None),
        check_vma=False,
    )
```
